512 devices in a mesh: gx: 8 (over x, core), gy: 16 (over z), gz: 4 (over y).
Axes of the slice: x: 4, y: 4, z: 16, core: 2. Of those that a mesh axis runs over, the one named last changes fastest.
Arguments:
- displacement: float32 [3, 32, 256, 512], P(None, 'gx', 'gy', 'gz'), may hold values from -6 to 6
- density: float32 [32, 256, 512], P('gx', 'gy', 'gz'), may hold values from 0.3 to 1
- solid: int32 [32, 256, 512], P('gx', 'gy', 'gz'), may hold values from 0 to 1, as said below
- material: int32 [32, 256, 512], P('gx', 'gy', 'gz'), may hold values from 0 to 3
- fixed: int32 [32, 256, 512], P('gx', 'gy', 'gz'), may hold values 0 or 1
Outputs:
- adjoint: float32 [3, 32, 256, 512], P(None, 'gx', 'gy', 'gz')
- sensitivity: float32 [32, 256, 512], P('gx', 'gy', 'gz')
The draws below stay inside these ranges and needn't reach their ends.
Inputs may be any that keep to these rules, and one draw needn't show every extreme that they name: 1 marks a solid element, 0 a void one.
All inputs are finite; a program needn't handle non-finite values. No bound on the sum of `fixed` on one device may be relied on, other than what follows from the above.
Results may differ from the reference program's by a relative error of at most 0.0003.
Values sent between devices are 32-bit elements; how exact they have to be, the bound alone decides.
A program may use at most 64 MiB of HBM per device.

```python
import jax
import jax.numpy as jnp
import numpy as np
from jax import lax

NX = 32
NY = 256
NZ = 512


def draw_solid(key, part):
    key = jax.random.fold_in(key, 7)
    level = 250 + 650 * jnp.arange(NY, dtype=jnp.int32) // NY
    ticket = jax.random.randint(key, (NX, NY, NZ), 0, 1000)
    return (ticket < level[None, :, None]).astype(jnp.int32)


def touch_ends(drawn, stream_key, least, largest):
    spot = [jax.random.randint(jax.random.fold_in(stream_key, axis), (), 0, length) for axis, length in enumerate(drawn.shape)]
    longest = drawn.shape.index(max(drawn.shape))
    neighbour = spot[:longest] + [(spot[longest] + 1) % drawn.shape[longest]] + spot[longest + 1:]
    return drawn.at[tuple(spot)].set(least).at[tuple(neighbour)].set(largest)


def block_levels(own_key, dims, shards, low, top_value):
    factor_of, own = 1.0, jax.random.fold_in(own_key, 6)
    for dim, shards_of in shards:
        heights = jnp.exp(jax.random.uniform(jax.random.fold_in(own, dim), (shards_of,), jnp.float32, low / len(shards), top_value / len(shards)))
        factor_of = factor_of * jnp.repeat(heights, dims[dim] // shards_of).reshape([-1 if axis == dim else 1 for axis in range(len(dims))])
    return factor_of


def centred(stream_key, extent, width, bound, cuts=(), kind=jnp.bfloat16):
    values = width * jax.random.normal(stream_key, extent, jnp.float32)
    if cuts:
        values = values * block_levels(stream_key, extent, cuts, -0.22, 0.18)
    return jnp.clip(values, -bound, bound).astype(kind)


def setup_inputs(seed: int = 0) -> dict:
    arg_keys = jax.random.split(jax.random.key(seed), 6)
    displacement = centred(arg_keys[0], (3, NX, NY, NZ), 1.0, 6.0, ((1, 8), (2, 16), (3, 4)), jnp.float32)
    density = jnp.clip(0.3 + 0.7 * jax.random.uniform(arg_keys[1], (NX, NY, NZ), jnp.float32) ** block_levels(arg_keys[1], (NX, NY, NZ), ((0, 8), (1, 16), (2, 4)), -0.2, 0.2), 0.3, 1.0)
    solid = draw_solid(jax.random.fold_in(arg_keys[5], 71), 0)
    material = touch_ends(jax.random.randint(arg_keys[3], (NX, NY, NZ), 0, 4), jax.random.fold_in(arg_keys[3], 1), 0, 3).astype(jnp.int32)
    fixed = touch_ends((jax.random.randint(arg_keys[4], (NX, NY, NZ), 0, 8) < 1).astype(jnp.int32), jax.random.fold_in(arg_keys[4], 1), 0, 1)
    return {"displacement": displacement, "density": density, "solid": solid, "material": material, "fixed": fixed}


POISSON = 0.3
VOID_FLOOR = 0.001
MODULI = (1.0, 0.7, 0.45, 0.25)

def lame_pair():
    first = POISSON / ((1.0 + POISSON) * (1.0 - 2.0 * POISSON))
    shear = 1.0 / (2.0 * (1.0 + POISSON))
    return (first, shear)

def corner_signs():
    return [(2 * a - 1, 2 * b - 1, 2 * c - 1) for a in (0, 1) for b in (0, 1) for c in (0, 1)]

def element_table():
    first, shear = lame_pair()
    elastic = np.zeros((6, 6))
    elastic[:3, :3] = first
    for index in range(3):
        elastic[index, index] += 2.0 * shear
        elastic[index + 3, index + 3] = shear
    point = 1.0 / np.sqrt(3.0)
    matrix = np.zeros((24, 24))
    for xi in (-point, point):
        for eta in (-point, point):
            for zeta in (-point, point):
                strain = np.zeros((6, 24))
                for index, signs in enumerate(corner_signs()):
                    sa, sb, sc = signs
                    gradx = 2.0 * sa * (1 + sb * eta) * (1 + sc * zeta) / 8.0
                    grady = 2.0 * sb * (1 + sa * xi) * (1 + sc * zeta) / 8.0
                    gradz = 2.0 * sc * (1 + sa * xi) * (1 + sb * eta) / 8.0
                    strain[0, index] = gradx
                    strain[1, 8 + index] = grady
                    strain[2, 16 + index] = gradz
                    strain[3, 8 + index] = gradz
                    strain[3, 16 + index] = grady
                    strain[4, index] = gradz
                    strain[4, 16 + index] = gradx
                    strain[5, index] = grady
                    strain[5, 8 + index] = gradx
                matrix += strain.T @ elastic @ strain / 8.0
    return matrix

def chebyshev_constants():
    rowsum = float(np.max(np.sum(np.abs(element_table()), axis=1)))
    upper = max(2.0, 8.0 * max(MODULI) * rowsum)
    lower = upper / 20.0
    theta = (upper + lower) / 2.0
    delta = (upper - lower) / 2.0
    sigma = theta / delta
    rho_zero = 1.0 / sigma
    rho_one = 1.0 / (2.0 * sigma - rho_zero)
    rho_two = 1.0 / (2.0 * sigma - rho_one)
    return (theta, delta, rho_zero, rho_one, rho_two)

def class_modulus(material):
    total = jnp.zeros(material.shape, jnp.float32)
    for index in range(4):
        total = total + jnp.where(material == index, MODULI[index], 0.0).astype(jnp.float32)
    return total

def corner_list(field):
    s0, s1, s2 = field.shape
    return [field[a:a + s0 - 1, b:b + s1 - 1, c:c + s2 - 1] for a in (0, 1) for b in (0, 1) for c in (0, 1)]

def assemble(values):
    n0, n1, n2 = values[0].shape
    total = None
    index = 0
    for a in (0, 1):
        for b in (0, 1):
            for c in (0, 1):
                piece = values[index][1 - a:1 - a + n0 - 1, 1 - b:1 - b + n1 - 1, 1 - c:1 - c + n2 - 1]
                total = piece if total is None else total + piece
                index += 1
    return total

def node_share(values):
    return assemble([values] * 8)

def gradient(component):
    corners = corner_list(component)
    signs = corner_signs()
    result = []
    for axis_number in range(3):
        total = None
        for index in range(8):
            piece = signs[index][axis_number] * corners[index]
            total = piece if total is None else total + piece
        result.append(0.25 * total)
    return result

def element_response(disp, modulus):
    grads = [gradient(disp[comp]) for comp in range(3)]
    exx, eyy, ezz = (grads[0][0], grads[1][1], grads[2][2])
    gyz = grads[1][2] + grads[2][1]
    gxz = grads[0][2] + grads[2][0]
    gxy = grads[0][1] + grads[1][0]
    first, shear = lame_pair()
    trace = exx + eyy + ezz
    sxx = first * trace + 2.0 * shear * exx
    syy = first * trace + 2.0 * shear * eyy
    szz = first * trace + 2.0 * shear * ezz
    syz, sxz, sxy = (shear * gyz, shear * gxz, shear * gxy)
    unit = sxx * sxx + syy * syy + szz * szz - sxx * syy - syy * szz - szz * sxx + 3.0 * (syz * syz + sxz * sxz + sxy * sxy)
    squared = modulus * modulus * unit
    power_two = squared * squared
    power_three = power_two * squared
    power_four = power_two * power_two
    hxx = 2.0 * sxx - syy - szz
    hyy = 2.0 * syy - sxx - szz
    hzz = 2.0 * szz - sxx - syy
    htrace = hxx + hyy + hzz
    weight = 4.0 * power_three * modulus * modulus
    wxx = weight * (first * htrace + 2.0 * shear * hxx)
    wyy = weight * (first * htrace + 2.0 * shear * hyy)
    wzz = weight * (first * htrace + 2.0 * shear * hzz)
    wyz = weight * shear * 6.0 * syz
    wxz = weight * shear * 6.0 * sxz
    wxy = weight * shear * 6.0 * sxy
    matrix = [[wxx, wxy, wxz], [wxy, wyy, wyz], [wxz, wyz, wzz]]
    signs = corner_signs()
    loads = []
    for comp in range(3):
        values = []
        for index in range(8):
            total = 0.25 * (signs[index][0] * matrix[comp][0] + signs[index][1] * matrix[comp][1] + signs[index][2] * matrix[comp][2])
            values.append(total)
        loads.append(assemble(values))
    return (power_four, power_three, unit, jnp.stack(loads))

def stiffness_apply(field, modulus, table):
    outputs = []
    for row in range(3):
        accum = None
        for col in range(3):
            stacked = jnp.stack(corner_list(field[col]))
            term = jnp.einsum('kj,jxyz->kxyz', table[row * 8:(row + 1) * 8, col * 8:(col + 1) * 8], stacked, precision=lax.Precision.HIGHEST)
            accum = term if accum is None else accum + term
        outputs.append(assemble(accum * modulus[None]))
    return jnp.stack(outputs)

def operator(field, free, modulus, table):
    inner = free[1:-1, 1:-1, 1:-1]
    applied = stiffness_apply(field * free[None], modulus, table)
    return inner[None] * applied + (1.0 - inner[None]) * field[:, 1:-1, 1:-1, 1:-1]

def energy(adjoint, disp, table):
    total = None
    for row in range(3):
        accum = None
        for col in range(3):
            stacked = jnp.stack(corner_list(disp[col]))
            term = jnp.einsum('kj,jxyz->kxyz', table[row * 8:(row + 1) * 8, col * 8:(col + 1) * 8], stacked, precision=lax.Precision.HIGHEST)
            accum = term if accum is None else accum + term
        part = lax.optimization_barrier(jnp.sum(jnp.stack(corner_list(adjoint[row])) * accum, axis=0))
        total = part if total is None else total + part
    return total

def reference(displacement, density, solid, material, fixed):
    table = jnp.asarray(element_table(), jnp.float32)
    theta, delta, rho_zero, rho_one, rho_two = chebyshev_constants()
    free = 1.0 - fixed.astype(jnp.float32)
    stiff = class_modulus(material) * (VOID_FLOOR + (1.0 - VOID_FLOOR) * solid.astype(jnp.float32))
    disp = displacement * free[None]

    def widen(field):
        return jnp.pad(field, ((0, 0), (1, 1), (1, 1), (1, 1)))
    disp_padded = widen(disp)
    dens_padded = jnp.pad(density, 1)
    free_padded = jnp.pad(free, 1)
    stiff_padded = jnp.pad(stiff, 1)
    elem_density = sum(corner_list(dens_padded)) / 8.0
    elem_stiff = stiff_padded[:-1, :-1, :-1]
    modulus = elem_density * elem_density * elem_density * elem_stiff
    power_four, power_three, unit, load = element_response(disp_padded, modulus)
    total = jnp.sum(power_four[1:, 1:, 1:])
    mean = total / float(NX * NY * NZ)
    aggregate = mean ** 0.125
    scale = aggregate / (8.0 * mean)
    rhs = scale * (free[None] * load)
    first_dir = rhs / theta
    resid_one = rhs - operator(widen(first_dir), free_padded, modulus, table)
    second_dir = rho_one * rho_zero * first_dir + 2.0 * rho_one / delta * resid_one
    resid_two = resid_one - operator(widen(second_dir), free_padded, modulus, table)
    third_dir = rho_two * rho_one * second_dir + 2.0 * rho_two / delta * resid_two
    adjoint = first_dir + second_dir + third_dir
    work = energy(widen(adjoint), disp_padded, table)
    growth = 3.0 * elem_density * elem_density * elem_stiff
    per_element = growth * (scale * 8.0 * power_three * modulus * unit - work)
    sensitivity = node_share(per_element) / 8.0
    return (adjoint, sensitivity)
```

```python
import functools
import itertools

import jax
import jax.numpy as jnp
import numpy as np
from jax import lax
from jax.experimental import pallas as pl
from jax.experimental.pallas import tpu as pltpu
from jax.sharding import PartitionSpec as P

POISSON = 0.3
VOID_FLOOR = 0.001
MODULI = (1.0, 0.7, 0.45, 0.25)
MESH = pl.DeviceIdType.MESH
AXES = ("gx", "gy", "gz")

BX, BY, BZ = 4, 16, 128
W = 4
NP = BX + 2 * W
ROWS = 32
CH = 3


def lame_pair():
    first = POISSON / ((1.0 + POISSON) * (1.0 - 2.0 * POISSON))
    shear = 1.0 / (2.0 * (1.0 + POISSON))
    return (first, shear)


def corner_signs():
    return [(2 * a - 1, 2 * b - 1, 2 * c - 1) for a in (0, 1) for b in (0, 1) for c in (0, 1)]


def element_table():
    first, shear = lame_pair()
    elastic = np.zeros((6, 6))
    elastic[:3, :3] = first
    for index in range(3):
        elastic[index, index] += 2.0 * shear
        elastic[index + 3, index + 3] = shear
    point = 1.0 / np.sqrt(3.0)
    matrix = np.zeros((24, 24))
    for xi in (-point, point):
        for eta in (-point, point):
            for zeta in (-point, point):
                strain = np.zeros((6, 24))
                for index, signs in enumerate(corner_signs()):
                    sa, sb, sc = signs
                    gradx = 2.0 * sa * (1 + sb * eta) * (1 + sc * zeta) / 8.0
                    grady = 2.0 * sb * (1 + sa * xi) * (1 + sc * zeta) / 8.0
                    gradz = 2.0 * sc * (1 + sa * xi) * (1 + sb * eta) / 8.0
                    strain[0, index] = gradx
                    strain[1, 8 + index] = grady
                    strain[2, 16 + index] = gradz
                    strain[3, 8 + index] = gradz
                    strain[3, 16 + index] = grady
                    strain[4, index] = gradz
                    strain[4, 16 + index] = gradx
                    strain[5, index] = grady
                    strain[5, 8 + index] = gradx
                matrix += strain.T @ elastic @ strain / 8.0
    return matrix


def chebyshev_constants():
    rowsum = float(np.max(np.sum(np.abs(element_table()), axis=1)))
    upper = max(2.0, 8.0 * max(MODULI) * rowsum)
    lower = upper / 20.0
    theta = (upper + lower) / 2.0
    delta = (upper - lower) / 2.0
    sigma = theta / delta
    rho_zero = 1.0 / sigma
    rho_one = 1.0 / (2.0 * sigma - rho_zero)
    rho_two = 1.0 / (2.0 * sigma - rho_one)
    return (theta, delta, rho_zero, rho_one, rho_two)


HALO = [d for d in itertools.product((-1, 0, 1), repeat=3) if d != (0, 0, 0)]
HALO.sort(key=lambda d: (d[2] != 0, abs(d[0]) + abs(d[1]) + abs(d[2])))


def partners(sizes):
    nx, ny, nz = sizes

    def far(d):
        return sum(min(o % n, -o % n) for o, n in zip(d, sizes))

    plane = [(a, 0, c) for a in range(nx) for c in range(nz) if (a, c) != (0, 0)]
    ring = [(0, b, 0) for b in range(1, ny)]
    return sorted(plane, key=far, reverse=True), sorted(ring, key=far, reverse=True)


GREETED = [(4, 0, 0), (4, 0, 2), (0, 4, 0), (0, -4, 0), (0, 7, 0), (0, -7, 0)]


def lanes():
    return lax.broadcasted_iota(jnp.int32, (2, 8, 128), 2)


def swapped(x):
    return jnp.stack([x[1], x[0]])


def z_next(x):
    r = pltpu.roll(x, 127, 2)
    return jnp.where(lanes() == 127, swapped(r), r)


def z_prev(x):
    r = pltpu.roll(x, 1, 2)
    return jnp.where(lanes() == 0, swapped(r), r)


def y_transform(ref, comp, plane, t):
    a = ref[comp, plane, :, 8 * t : 8 * t + 8, :]
    b = ref[comp, plane, :, 8 * t + 1 : 8 * t + 9, :]
    return a + b, b - a


def full_transform(ref, comp, plane, t):
    s, d = y_transform(ref, comp, plane, t)
    sn, dn = z_next(s), z_next(d)
    return [s + sn, sn - s, d + dn, dn - d]


def central_transform(ref, comp, plane, t):
    s, d = y_transform(ref, comp, plane, t)
    sn, dn = z_next(s), z_next(d)
    return [s + sn, sn - s, d + dn]


def central_gradients(old, new):
    return [new[0] - old[0], old[2] + new[2], old[1] + new[1]]


def stress_of(grads):
    first, shear = lame_pair()
    exx, eyy, ezz = grads[0][0], grads[1][1], grads[2][2]
    base = first * (exx + eyy + ezz)
    sxx, syy, szz = base + 2.0 * shear * exx, base + 2.0 * shear * eyy, base + 2.0 * shear * ezz
    syz = shear * (grads[1][2] + grads[2][1])
    sxz = shear * (grads[0][2] + grads[2][0])
    sxy = shear * (grads[0][1] + grads[1][0])
    return sxx, syy, szz, syz, sxz, sxy


def unit_of(s):
    sxx, syy, szz, syz, sxz, sxy = s
    return (
        sxx * sxx + syy * syy + szz * szz - sxx * syy - syy * szz - szz * sxx
        + 3.0 * (syz * syz + sxz * sxz + sxy * sxy)
    )


def element_modes(old, new):
    ss, sd, ds, dd = zip(old, new)
    return {
        "DSS": ss[1] - ss[0], "SSD": sd[0] + sd[1], "DSD": sd[1] - sd[0], "SDS": ds[0] + ds[1],
        "DDS": ds[1] - ds[0], "SDD": dd[0] + dd[1], "DDD": dd[1] - dd[0],
    }


def element_forces(modes):
    first, shear = lame_pair()
    u, v, w = modes
    s = stress_of([[m["DSS"], m["SDS"], m["SSD"]] for m in (u, v, w)])
    sxx, syy, szz, syz, sxz, sxy = [x * (1.0 / 16.0) for x in s]
    own, cross = (first + 3.0 * shear) / 48.0, first / 48.0
    twist, cube = shear / 48.0, (first + 4.0 * shear) / 144.0

    def pair(a, b):
        return own * a + cross * b, cross * a + own * b

    u_xy, w_yz = pair(u["DDS"], w["SDD"])
    u_xz, v_yz = pair(u["DSD"], v["SDD"])
    v_xy, w_xz = pair(v["DDS"], w["DSD"])
    every = u["SDD"] + v["DSD"] + w["DDS"]
    return [
        {"DSS": sxx, "SDS": sxy, "SSD": sxz, "DDS": u_xy, "DSD": u_xz,
         "SDD": twist * (every + u["SDD"]), "DDD": cube * u["DDD"]},
        {"DSS": sxy, "SDS": syy, "SSD": syz, "DDS": v_xy, "SDD": v_yz,
         "DSD": twist * (every + v["DSD"]), "DDD": cube * v["DDD"]},
        {"DSS": sxz, "SDS": syz, "SSD": szz, "SDD": w_yz, "DSD": w_xz,
         "DDS": twist * (every + w["DDS"]), "DDD": cube * w["DDD"]},
    ]


def y_gather(value, kept):
    r = pltpu.roll(value, 1, 1)
    if kept is None:
        return r, r
    rows = lax.broadcasted_iota(jnp.int32, (2, 8, 128), 1)
    return jnp.where(rows == 0, kept, r), r


def kernel(sizes, disp_in, dens_in, solid_in, mat_in, fixed_in, adj_out, sens_out,
           disp_v, dens_v, solid_v, mat_v, fixed_v, own, ylow, yhigh, zlow, zhigh, zlow_y, zhigh_y,
           rx, ry, rz, ryz, fld, mod_e, grow, lead, rhs, v0, fv0, v1, fv1, adj, sens, carry_t, carry_p,
           src1, land1, src2, land2, in_sem, send_sem, recv_sem, s1, r1, s2, r2):
    position = [lax.axis_index(a) for a in AXES]

    def at(d):
        return tuple(lax.rem(p + (o % n), n) if o % n else p for p, o, n in zip(position, d, sizes))

    plane, ring = partners(sizes)
    theta, delta, rho_zero, rho_one, rho_two = chebyshev_constants()

    loads = [
        pltpu.make_async_copy(src, dst, in_sem.at[n])
        for n, (src, dst) in enumerate(
            ((disp_in, disp_v), (dens_in, dens_v), (solid_in, solid_v), (mat_in, mat_v), (fixed_in, fixed_v))
        )
    ]
    for copy in loads:
        copy.start()
    barrier = pltpu.get_barrier_semaphore()
    greeted = HALO + GREETED
    for d in greeted:
        pl.semaphore_signal(barrier, inc=1, device_id=at(d), device_id_type=MESH)

    zero = jnp.zeros((2, 8, 128), jnp.float32)

    def clear(p, _):
        for f in range(6):
            fld[f, p, :, 24:32, :] = zero
        for c in range(3):
            fv0[c, p, :, 24:32, :] = zero
            fv1[c, p, :, 24:32, :] = zero
            adj[c, p, :, 24:32, :] = zero
        return 0

    lax.fori_loop(0, NP, clear, 0)
    for copy in loads:
        copy.wait()

    free = 1.0 - fixed_v[...].astype(jnp.float32)
    own[4] = free
    own[3] = dens_v[...]
    for c in range(3):
        own[c] = disp_v[c] * free
    material = mat_v[...]
    scale_class = jnp.zeros(material.shape, jnp.float32)
    for index in range(4):
        scale_class = scale_class + jnp.where(material == index, MODULI[index], 0.0).astype(jnp.float32)
    own[5] = scale_class * (VOID_FLOOR + (1.0 - VOID_FLOOR) * solid_v[...].astype(jnp.float32))

    lane16 = lax.broadcasted_iota(jnp.int32, (16, 128), 1)
    low = jnp.zeros((16, 128), jnp.float32)
    high = jnp.zeros((16, 128), jnp.float32)
    for f in range(6):
        for p in range(BX):
            group = 4 * (BX * f + p)
            block = own[f, p]
            mine = (lane16 >= group) & (lane16 < group + 4)
            low = jnp.where(mine, pltpu.roll(block, group, 1) if group else block, low)
            high = jnp.where(mine, pltpu.roll(block, group + 4, 1), high)
            half = 4 * (p % 2)
            ylow[f, p // 2, half : half + 4, :] = block[0:4]
            yhigh[f, p // 2, half : half + 4, :] = block[12:16]
    zlow[...] = low
    zhigh[...] = high
    for ref, value in ((zlow_y, low), (zhigh_y, high)):
        ref[0:4, :] = value[0:4]
        ref[4:8, :] = value[12:16]

    pl.semaphore_wait(barrier, len(greeted))
    halos = []
    for n, (dx, dy, dz) in enumerate(HALO):
        sx, sy, sz = 1 - dx, (1 - dy) // 2, (1 - dz) // 2
        if dz == 0 and dy == 0:
            src, dst = own, rx.at[sx // 2]
        elif dz == 0:
            src, dst = (yhigh if dy > 0 else ylow), ry.at[sx, sy]
        elif dy == 0:
            src, dst = (zhigh if dz > 0 else zlow), rz.at[sx, sz]
        else:
            src, dst = (zhigh_y if dz > 0 else zlow_y), ryz.at[sx, sy, sz]
        copy = pltpu.make_async_remote_copy(
            src_ref=src, dst_ref=dst, send_sem=send_sem.at[n], recv_sem=recv_sem.at[n],
            device_id=at((dx, dy, dz)), device_id_type=MESH,
        )
        copy.start()
        halos.append(copy)
    for copy in halos:
        copy.wait_recv()

    def inside(axis, o):
        if o == 0:
            return 1.0
        edge = 0 if o < 0 else sizes[axis] - 1
        return jnp.where(position[axis] == edge, 0.0, 1.0).astype(jnp.float32)

    half_lanes16 = lane16 < 64
    half_lanes8 = lax.broadcasted_iota(jnp.int32, (8, 128), 1) < 64

    def unpack(f, _):
        for sx in range(3):
            fx = inside(0, sx - 1)
            for p in range(BX):
                q = BX * sx + p
                block = own[f, p] if sx == 1 else rx[sx // 2, f, p] * fx
                fld[f, q, 0, 4:20, :] = block
                half = 4 * (p % 2)
                for sy, rows in ((0, 0), (1, 20)):
                    part = ry[sx, sy, f, p // 2, half : half + 4, :]
                    fld[f, q, 0, rows : rows + 4, :] = part * (fx * inside(1, 2 * sy - 1))
                group = 4 * (BX * f + p)
                below, above = rz[sx, 0] * (fx * inside(2, -1)), rz[sx, 1] * (fx * inside(2, 1))
                to_low, to_high = lax.rem(256 - group, 128), lax.rem(256 - 4 - group, 128)
                fld[f, q, 1, 4:20, :] = jnp.where(
                    half_lanes16, pltpu.roll(above, to_low, 1), pltpu.roll(below, to_high, 1)
                )
                for sy, rows in ((0, 0), (1, 20)):
                    fxy = fx * inside(1, 2 * sy - 1)
                    below, above = ryz[sx, sy, 0] * (fxy * inside(2, -1)), ryz[sx, sy, 1] * (fxy * inside(2, 1))
                    edge = jnp.where(half_lanes8, pltpu.roll(above, to_low, 1), pltpu.roll(below, to_high, 1))
                    fld[f, q, 1, rows : rows + 4, :] = edge[4:8] if sy == 0 else edge[0:4]
        return 0

    lax.fori_loop(0, 6, unpack, 0)

    def own_total(e, acc):
        for start in (4, 12):
            sides = []
            for side in range(2):
                parts = []
                for c in range(4):
                    a = fld[c, e + side, :, start : start + 8, :]
                    b = fld[c, e + side, :, start + 1 : start + 9, :]
                    s, d = a + b, b - a
                    sn, dn = z_next(s), z_next(d)
                    parts.append([(s + sn)[0], (sn - s)[0], (d + dn)[0]])
                sides.append(parts)
            old, new = sides
            grads = [[0.25 * g for g in central_gradients(old[c], new[c])] for c in range(3)]
            rho = (old[3][0] + new[3][0]) * 0.125
            modulus = rho * rho * rho * fld[5, e, 0, start : start + 8, :]
            q = modulus * modulus * unit_of(stress_of(grads))
            q = q * q
            acc = acc + q * q
        return acc

    partial = lax.fori_loop(W, W + BX, own_total, jnp.zeros((8, 128), jnp.float32))
    src1[...] = partial
    sums1 = []
    for n, d in enumerate(plane):
        copy = pltpu.make_async_remote_copy(
            src_ref=src1, dst_ref=land1.at[n], send_sem=s1.at[n], recv_sem=r1.at[n],
            device_id=at(d), device_id_type=MESH,
        )
        copy.start()
        sums1.append(copy)

    kinds = ("SS", "SD", "DS", "DD")

    def scatter(t, forces, kept, names):
        result, keep = [], []
        for c in range(3):
            by = {}
            for i, k in enumerate(kinds):
                s, d = forces[c].get("S" + k), forces[c].get("D" + k)
                if s is None and d is None:
                    continue
                if s is None:
                    lower, upper = -d, d
                elif d is None:
                    lower, upper = s, s
                else:
                    lower, upper = s - d, s + d
                by[k] = lower + carry_p[t, 4 * c + i]
                carry_p[t, 4 * c + i] = upper
            rows = []
            for k in ("S", "D"):
                s, d = by[k + "S"], by.get(k + "D")
                if d is None:
                    rows.append(s + z_prev(s))
                else:
                    rows.append((s - d) + z_prev(s + d))
            down, r = y_gather(rows[0] + rows[1], None if kept is None else kept[c])
            result.append((rows[0] - rows[1]) + down)
            keep.append(r)
        return result, keep

    def clear_carry():
        def body(i, _):
            for t in range(CH):
                carry_p[t, i] = zero
            return 0
        lax.fori_loop(0, 12, body, 0)

    def chunk(t):
        return slice(8 * t, 8 * t + 8)

    clear_carry()
    for t in range(CH):
        for c in range(4):
            for i, value in enumerate(central_transform(fld, c, 0, t)):
                carry_t[t, 4 * c + i] = value

    def stage_one(e, _):
        kept = None
        first, shear = lame_pair()
        for t in range(CH):
            grads = []
            for c in range(3):
                new = central_transform(fld, c, e + 1, t)
                old = [carry_t[t, 4 * c + i] for i in range(3)]
                for i, value in enumerate(new):
                    carry_t[t, 4 * c + i] = value
                grads.append([0.25 * g for g in central_gradients(old, new)])
            s, _d = y_transform(fld, 3, e + 1, t)
            mass = s + z_next(s)
            rho = (carry_t[t, 12] + mass) * 0.125
            carry_t[t, 12] = mass
            stiff = fld[5, e, :, chunk(t), :]
            rho_stiff = rho * rho * stiff
            modulus = rho_stiff * rho
            growth = 3.0 * rho_stiff
            mod_e[e, :, chunk(t), :] = modulus
            grow[e, :, chunk(t), :] = growth
            stress = stress_of(grads)
            unit = unit_of(stress)
            square = modulus * modulus
            q = square * unit
            q3 = q * q * q
            lead[e, :, chunk(t), :] = growth * (8.0 * q3 * modulus * unit)
            sxx, syy, szz, syz, sxz, sxy = stress
            weight = q3 * square
            tr = sxx + syy + szz
            hxx, hyy, hzz = 3.0 * sxx - tr, 3.0 * syy - tr, 3.0 * szz - tr
            base = first * (hxx + hyy + hzz)
            wxx = weight * (base + 2.0 * shear * hxx)
            wyy = weight * (base + 2.0 * shear * hyy)
            wzz = weight * (base + 2.0 * shear * hzz)
            skew = weight * (6.0 * shear)
            wyz, wxz, wxy = skew * syz, skew * sxz, skew * sxy
            forces = [
                {"DSS": wxx, "SDS": wxy, "SSD": wxz},
                {"DSS": wxy, "SDS": wyy, "SSD": wyz},
                {"DSS": wxz, "SDS": wyz, "SSD": wzz},
            ]
            load, kept = scatter(t, forces, kept, None)
            free = fld[4, e, :, chunk(t), :]
            for c in range(3):
                r = free * load[c]
                d = r * (1.0 / theta)
                rhs[c, e, :, chunk(t), :] = r
                v0[c, e, :, chunk(t), :] = d
                fv0[c, e, :, chunk(t), :] = free * d
        return 0

    lax.fori_loop(0, NP - 1, stage_one, 0)

    def apply_sweep(ref, first_plane, last_plane, node):
        clear_carry()
        for t in range(CH):
            for c in range(3):
                for i, value in enumerate(full_transform(ref, c, first_plane, t)):
                    carry_t[t, 4 * c + i] = value

        def body(e, _):
            kept = None
            for t in range(CH):
                modes = []
                for c in range(3):
                    new = full_transform(ref, c, e + 1, t)
                    old = [carry_t[t, 4 * c + i] for i in range(4)]
                    for i, value in enumerate(new):
                        carry_t[t, 4 * c + i] = value
                    modes.append(element_modes(old, new))
                modulus = mod_e[e, :, chunk(t), :]
                forces = [{k: modulus * f for k, f in g.items()} for g in element_forces(modes)]
                applied, kept = scatter(t, forces, kept, None)
                free = fld[4, e, :, chunk(t), :]
                for c in range(3):
                    node(c, e, t, free, applied[c])
            return 0

        lax.fori_loop(first_plane, last_plane, body, 0)

    def node_two(c, e, t, free, applied):
        d = v0[c, e, :, chunk(t), :]
        r = rhs[c, e, :, chunk(t), :] - (free * applied + (1.0 - free) * d)
        new = (rho_one * rho_zero) * d + (2.0 * rho_one / delta) * r
        rhs[c, e, :, chunk(t), :] = r
        v1[c, e, :, chunk(t), :] = new
        fv1[c, e, :, chunk(t), :] = free * new

    apply_sweep(fv0, 1, NP - 2, node_two)

    for copy in sums1:
        copy.wait_recv()
    total = src1[...]
    for n in range(len(plane)):
        total = total + land1[n]
    src2[...] = total
    sums2 = []
    for n, d in enumerate(ring):
        copy = pltpu.make_async_remote_copy(
            src_ref=src2, dst_ref=land2.at[n], send_sem=s2.at[n], recv_sem=r2.at[n],
            device_id=at(d), device_id_type=MESH,
        )
        copy.start()
        sums2.append(copy)

    def node_three(c, e, t, free, applied):
        d = v1[c, e, :, chunk(t), :]
        r = rhs[c, e, :, chunk(t), :] - (free * applied + (1.0 - free) * d)
        new = (rho_two * rho_one) * d + (2.0 * rho_two / delta) * r
        adj[c, e, :, chunk(t), :] = v0[c, e, :, chunk(t), :] + d + new

    apply_sweep(fv1, 2, NP - 3, node_three)

    for t in range(CH):
        carry_p[t, 0] = zero
        for c in range(3):
            for i, value in enumerate(full_transform(adj, c, 3, t)):
                carry_t[t, 4 * c + i] = value
            for i, value in enumerate(full_transform(fld, c, 3, t)):
                carry_t[t, 12 + 4 * c + i] = value

    def stage_four(e, _):
        kept = None
        for t in range(CH):
            modes = []
            for ref, base in ((adj, 0), (fld, 12)):
                group = []
                for c in range(3):
                    new = full_transform(ref, c, e + 1, t)
                    old = [carry_t[t, base + 4 * c + i] for i in range(4)]
                    for i, value in enumerate(new):
                        carry_t[t, base + 4 * c + i] = value
                    group.append(element_modes(old, new))
                modes.append(group)
            forces = element_forces(modes[1])
            work = None
            for a, f in zip(modes[0], forces):
                for k, value in f.items():
                    work = a[k] * value if work is None else work + a[k] * value
            g = lead[e, :, chunk(t), :] - grow[e, :, chunk(t), :] * work
            share = g + carry_p[t, 0]
            carry_p[t, 0] = g
            share = share + z_prev(share)
            down, kept = y_gather(share, kept)
            sens[e, chunk(t), :] = (share + down)[0]
        return 0

    lax.fori_loop(3, W + BX, stage_four, 0)

    for copy in sums2:
        copy.wait_recv()
    total = src2[...]
    for n in range(len(ring)):
        total = total + land2[n]
    total = jnp.sum(jnp.sum(total, axis=0, keepdims=True), axis=1, keepdims=True)
    mean = total * (1.0 / float(BX * BY * BZ * sizes[0] * sizes[1] * sizes[2]))
    aggregate = jnp.sqrt(jnp.sqrt(jnp.sqrt(mean)))
    scale = jnp.broadcast_to(aggregate / (8.0 * mean), (8, 128))
    share = scale * 0.125
    for p in range(BX):
        for h in (0, 8):
            sens_out[p, h : h + 8, :] = share * sens[W + p, h + 4 : h + 12, :]
            for c in range(3):
                adj_out[c, p, h : h + 8, :] = scale * adj[c, W + p, 0, h + 4 : h + 12, :]

    for copy in halos + sums1 + sums2:
        copy.wait_send()


def local(sizes, displacement, density, solid, material, fixed):
    plane, ring = partners(sizes)
    f32, i32 = jnp.float32, jnp.int32
    vm = pltpu.VMEM
    dma = pltpu.SemaphoreType.DMA
    node = (3, NP, 2, ROWS, 128)
    scratch = [
        vm((3, BX, BY, BZ), f32), vm((BX, BY, BZ), f32), vm((BX, BY, BZ), i32), vm((BX, BY, BZ), i32), vm((BX, BY, BZ), i32),
        vm((6, BX, BY, BZ), f32), vm((6, 2, 8, 128), f32), vm((6, 2, 8, 128), f32),
        vm((16, 128), f32), vm((16, 128), f32), vm((8, 128), f32), vm((8, 128), f32),
        vm((2, 6, BX, BY, BZ), f32), vm((3, 2, 6, 2, 8, 128), f32), vm((3, 2, 16, 128), f32), vm((3, 2, 2, 8, 128), f32),
        vm((6, NP, 2, ROWS, 128), f32),
        vm((NP, 2, 24, 128), f32), vm((NP, 2, 24, 128), f32), vm((NP, 2, 24, 128), f32),
        vm(node, f32), vm(node, f32), vm(node, f32), vm(node, f32), vm(node, f32), vm(node, f32),
        vm((NP, 24, 128), f32),
        vm((CH, 24, 2, 8, 128), f32), vm((CH, 12, 2, 8, 128), f32),
        vm((8, 128), f32), vm((len(plane), 8, 128), f32), vm((8, 128), f32), vm((len(ring), 8, 128), f32),
        dma((5,)), dma((len(HALO),)), dma((len(HALO),)),
        dma((len(plane),)), dma((len(plane),)), dma((len(ring),)), dma((len(ring),)),
    ]
    return pl.pallas_call(
        functools.partial(kernel, sizes),
        out_shape=(jax.ShapeDtypeStruct((3, BX, BY, BZ), f32), jax.ShapeDtypeStruct((BX, BY, BZ), f32)),
        in_specs=[pl.BlockSpec(memory_space=pl.ANY)] * 5,
        out_specs=(pl.BlockSpec(memory_space=pltpu.VMEM), pl.BlockSpec(memory_space=pltpu.VMEM)),
        scratch_shapes=scratch,
        compiler_params=pltpu.CompilerParams(
            collective_id=0, has_side_effects=True, vmem_limit_bytes=40 * 1024 * 1024
        ),
    )(displacement, density, solid, material, fixed)


def solution(mesh):
    sizes = tuple(mesh.shape[a] for a in AXES)
    field = P(*AXES)
    vector = P(None, *AXES)
    return jax.shard_map(
        functools.partial(local, sizes),
        mesh=mesh,
        in_specs=(vector, field, field, field, field),
        out_specs=(vector, field),
        check_vma=False,
    )
```

```python
import functools
import itertools

import jax
import jax.numpy as jnp
import numpy as np
from jax import lax
from jax.experimental import pallas as pl
from jax.experimental.pallas import tpu as pltpu
from jax.sharding import PartitionSpec as P

POISSON = 0.3
VOID_FLOOR = 0.001
MODULI = (1.0, 0.7, 0.45, 0.25)
MESH = pl.DeviceIdType.MESH
AXES = ("gx", "gy", "gz")

BX, BY, BZ = 4, 16, 128
W = 4
NP = BX + 2 * W
ROWS = 40
UNITS = 4
GROUP = 24


def lame_pair():
    first = POISSON / ((1.0 + POISSON) * (1.0 - 2.0 * POISSON))
    shear = 1.0 / (2.0 * (1.0 + POISSON))
    return (first, shear)


def corner_signs():
    return [(2 * a - 1, 2 * b - 1, 2 * c - 1) for a in (0, 1) for b in (0, 1) for c in (0, 1)]


def element_table():
    first, shear = lame_pair()
    elastic = np.zeros((6, 6))
    elastic[:3, :3] = first
    for index in range(3):
        elastic[index, index] += 2.0 * shear
        elastic[index + 3, index + 3] = shear
    point = 1.0 / np.sqrt(3.0)
    matrix = np.zeros((24, 24))
    for xi in (-point, point):
        for eta in (-point, point):
            for zeta in (-point, point):
                strain = np.zeros((6, 24))
                for index, signs in enumerate(corner_signs()):
                    sa, sb, sc = signs
                    gradx = 2.0 * sa * (1 + sb * eta) * (1 + sc * zeta) / 8.0
                    grady = 2.0 * sb * (1 + sa * xi) * (1 + sc * zeta) / 8.0
                    gradz = 2.0 * sc * (1 + sa * xi) * (1 + sb * eta) / 8.0
                    strain[0, index] = gradx
                    strain[1, 8 + index] = grady
                    strain[2, 16 + index] = gradz
                    strain[3, 8 + index] = gradz
                    strain[3, 16 + index] = grady
                    strain[4, index] = gradz
                    strain[4, 16 + index] = gradx
                    strain[5, index] = grady
                    strain[5, 8 + index] = gradx
                matrix += strain.T @ elastic @ strain / 8.0
    return matrix


def chebyshev_constants():
    rowsum = float(np.max(np.sum(np.abs(element_table()), axis=1)))
    upper = max(2.0, 8.0 * max(MODULI) * rowsum)
    lower = upper / 20.0
    theta = (upper + lower) / 2.0
    delta = (upper - lower) / 2.0
    sigma = theta / delta
    rho_zero = 1.0 / sigma
    rho_one = 1.0 / (2.0 * sigma - rho_zero)
    rho_two = 1.0 / (2.0 * sigma - rho_one)
    return (theta, delta, rho_zero, rho_one, rho_two)


HALO = [d for d in itertools.product((-1, 0, 1), repeat=3) if d != (0, 0, 0)]
FIRST = [(-1, -1, -1), (0, -1, -1), (-1, 0, -1), (-1, -1, 0), (-1, 0, 0), (0, 0, -1), (0, -1, 0)]
LATER = sorted((d for d in HALO if d not in FIRST), key=lambda d: (-abs(d[0]) - abs(d[1]) - abs(d[2])))


def partners(sizes):
    nx, ny, nz = sizes

    def far(d):
        return sum(min(o % n, -o % n) for o, n in zip(d, sizes))

    plane = [(a, 0, c) for a in range(nx) for c in range(nz) if (a, c) != (0, 0)]
    ring = [(0, b, 0) for b in range(1, ny)]
    return sorted(plane, key=far, reverse=True), sorted(ring, key=far, reverse=True)


GREETED = [(0, 7, 0), (0, -7, 0), (0, 4, 0), (0, -4, 0), (3, 0, 2), (-3, 0, 2), (3, 0, 0), (-3, 0, 0)]


def rows_of():
    return lax.broadcasted_iota(jnp.int32, (8, 128), 0)


def z_next(x):
    return pltpu.roll(x, 127, 1)


def z_prev(x):
    return pltpu.roll(x, 1, 1)


def unit_rows(t):
    return slice(32, 40) if t == 3 else slice(8 * t, 8 * t + 8)


def element_rows(t):
    return slice(8 * t, 8 * t + 8)


def y_transform(ref, comp, plane, t):
    a = ref[comp, plane, unit_rows(t), :]
    if t < 3:
        b = ref[comp, plane, 8 * t + 1 : 8 * t + 9, :]
    else:
        r = pltpu.roll(a, 7, 0)
        b = jnp.where(rows_of() == 7, pltpu.roll(r, 128 - GROUP, 1), r)
    return a + b, b - a


def full_transform(ref, comp, plane, t):
    s, d = y_transform(ref, comp, plane, t)
    sn, dn = z_next(s), z_next(d)
    return [s + sn, sn - s, d + dn, dn - d]


def central_transform(ref, comp, plane, t):
    s, d = y_transform(ref, comp, plane, t)
    sn, dn = z_next(s), z_next(d)
    return [s + sn, sn - s, d + dn]


def central_gradients(old, new):
    return [new[0] - old[0], old[2] + new[2], old[1] + new[1]]


def stress_of(grads):
    first, shear = lame_pair()
    exx, eyy, ezz = grads[0][0], grads[1][1], grads[2][2]
    base = first * (exx + eyy + ezz)
    sxx, syy, szz = base + 2.0 * shear * exx, base + 2.0 * shear * eyy, base + 2.0 * shear * ezz
    syz = shear * (grads[1][2] + grads[2][1])
    sxz = shear * (grads[0][2] + grads[2][0])
    sxy = shear * (grads[0][1] + grads[1][0])
    return sxx, syy, szz, syz, sxz, sxy


def unit_of(s):
    sxx, syy, szz, syz, sxz, sxy = s
    return (
        sxx * sxx + syy * syy + szz * szz - sxx * syy - syy * szz - szz * sxx
        + 3.0 * (syz * syz + sxz * sxz + sxy * sxy)
    )


def element_modes(old, new):
    ss, sd, ds, dd = zip(old, new)
    return {
        "DSS": ss[1] - ss[0], "SSD": sd[0] + sd[1], "DSD": sd[1] - sd[0], "SDS": ds[0] + ds[1],
        "DDS": ds[1] - ds[0], "SDD": dd[0] + dd[1], "DDD": dd[1] - dd[0],
    }


def element_forces(modes):
    first, shear = lame_pair()
    u, v, w = modes
    s = stress_of([[m["DSS"], m["SDS"], m["SSD"]] for m in (u, v, w)])
    sxx, syy, szz, syz, sxz, sxy = [x * (1.0 / 16.0) for x in s]
    own, cross = (first + 3.0 * shear) / 48.0, first / 48.0
    twist, cube = shear / 48.0, (first + 4.0 * shear) / 144.0

    def pair(a, b):
        return own * a + cross * b, cross * a + own * b

    u_xy, w_yz = pair(u["DDS"], w["SDD"])
    u_xz, v_yz = pair(u["DSD"], v["SDD"])
    v_xy, w_xz = pair(v["DDS"], w["DSD"])
    every = u["SDD"] + v["DSD"] + w["DDS"]
    return [
        {"DSS": sxx, "SDS": sxy, "SSD": sxz, "DDS": u_xy, "DSD": u_xz,
         "SDD": twist * (every + u["SDD"]), "DDD": cube * u["DDD"]},
        {"DSS": sxy, "SDS": syy, "SSD": syz, "DDS": v_xy, "SDD": v_yz,
         "DSD": twist * (every + v["DSD"]), "DDD": cube * v["DDD"]},
        {"DSS": sxz, "SDS": syz, "SSD": szz, "SDD": w_yz, "DSD": w_xz,
         "DDS": twist * (every + w["DDS"]), "DDD": cube * w["DDD"]},
    ]


def y_prev(value, kept, t):
    r = pltpu.roll(value, 1, 0)
    if t == 0:
        return r, r
    before = kept if t < 3 else pltpu.roll(r, GROUP, 1)
    return jnp.where(rows_of() == 0, before, r), r


def kernel(sizes, disp_in, dens_in, solid_in, mat_in, fixed_in, adj_out, sens_out,
           disp_v, dens_v, solid_v, mat_v, fixed_v, own, ylow, yhigh, zlow, zhigh, zlow_y, zhigh_y, yfirst,
           rx, ry, rz, ryz, rxf, ryf, strip, tm, tn, fld, mod_e, grow, lead, rhs, v0, fv0, v1, fv1, adj, sens, merged,
           carry_t, carry_p, src1, land1, src2, land2, in_sem, send_sem, recv_sem, s1, r1, s2, r2):
    position = [lax.axis_index(a) for a in AXES]

    def at(d):
        return tuple(lax.rem(p + (o % n), n) if o % n else p for p, o, n in zip(position, d, sizes))

    plane, ring = partners(sizes)
    theta, delta, rho_zero, rho_one, rho_two = chebyshev_constants()

    loads = [
        pltpu.make_async_copy(src, dst, in_sem.at[n])
        for n, (src, dst) in enumerate(
            ((disp_in, disp_v), (fixed_in, fixed_v), (dens_in, dens_v), (mat_in, mat_v), (solid_in, solid_v))
        )
    ]
    for copy in loads:
        copy.start()
    barrier = pltpu.get_barrier_semaphore()
    greeted = GREETED + LATER + FIRST
    for d in greeted:
        pl.semaphore_signal(barrier, inc=1, device_id=at(d), device_id_type=MESH)
    for copy in loads:
        copy.wait()

    free = 1.0 - fixed_v[...].astype(jnp.float32)
    own[4] = free
    own[3] = dens_v[...]
    for c in range(3):
        own[c] = disp_v[c] * free
    material = mat_v[...]
    scale_class = jnp.zeros(material.shape, jnp.float32)
    for index in range(4):
        scale_class = scale_class + jnp.where(material == index, MODULI[index], 0.0).astype(jnp.float32)
    own[5] = scale_class * (VOID_FLOOR + (1.0 - VOID_FLOOR) * solid_v[...].astype(jnp.float32))

    lane16 = lax.broadcasted_iota(jnp.int32, (16, 128), 1)
    lane8 = lax.broadcasted_iota(jnp.int32, (8, 128), 1)

    def pack_lanes(first_lane, ref, ref_y):
        packed = jnp.zeros((16, 128), jnp.float32)
        for f in range(6):
            for p in range(BX):
                group = 4 * (BX * f + p)
                shift = (group - first_lane) % 128
                block = own[f, p]
                packed = jnp.where(lane16 < group, packed, pltpu.roll(block, shift, 1) if shift else block)
        ref[...] = packed
        ref_y[0:4, :] = packed[0:4]
        ref_y[4:8, :] = packed[12:16]

    pack_lanes(0, zlow, zlow_y)
    for f in range(4):
        for p in range(BX):
            yfirst[BX * f + p : BX * f + p + 1, :] = own[f, p, 0:1, :]

    pl.semaphore_wait(barrier, len(greeted))

    def send(src, dst, d, sems, n, group):
        copy = pltpu.make_async_remote_copy(
            src_ref=src, dst_ref=dst, send_sem=sems[0].at[n], recv_sem=sems[1].at[n],
            device_id=at(d), device_id_type=MESH,
        )
        copy.start()
        group.append(copy)

    halo_sems = (send_sem, recv_sem)
    first, later = [], []
    for n, (dx, dy, dz) in enumerate(FIRST):
        sx = 1 - dx
        if dz:
            src, dst = (zlow_y, ryz.at[sx, 1, 1]) if dy else (zlow, rz.at[sx, 1])
        else:
            src, dst = (yfirst, ryf.at[sx - 1]) if dy else (own.at[pl.ds(0, 4), 0], rxf)
        send(src, dst, (dx, dy, dz), halo_sems, n, first)

    pack_lanes(124, zhigh, zhigh_y)
    for f in range(6):
        for p in range(BX):
            half = 4 * (p % 2)
            ylow[f, p // 2, half : half + 4, :] = own[f, p, 0:4, :]
            yhigh[f, p // 2, half : half + 4, :] = own[f, p, 12:16, :]
    rest = [d for d in HALO if d not in FIRST or d[2] == 0]
    rest.sort(key=lambda d: (d[2] != 0, d[1] != 0))
    for n, (dx, dy, dz) in enumerate(rest):
        sx, sy, sz = 1 - dx, (1 - dy) // 2, (1 - dz) // 2
        if dz == 0 and dy == 0:
            src, dst = own, rx.at[sx // 2]
        elif dz == 0:
            src, dst = (yhigh if dy > 0 else ylow), ry.at[sx, sy]
        elif dy == 0:
            src, dst = (zhigh if dz > 0 else zlow), rz.at[sx, sz]
        else:
            src, dst = (zhigh_y if dz > 0 else zlow_y), ryz.at[sx, sy, sz]
        send(src, dst, (dx, dy, dz), halo_sems, len(FIRST) + n, later)

    zero = jnp.zeros((8, 128), jnp.float32)

    def clear(p, _):
        for f in range(6):
            fld[f, p, 24:32, :] = zero
        for c in range(3):
            fv0[c, p, 24:32, :] = zero
            fv1[c, p, 24:32, :] = zero
            adj[c, p, 24:32, :] = zero
        return 0

    lax.fori_loop(0, NP, clear, 0)

    def inside(axis, o):
        if o == 0:
            return 1.0
        edge = 0 if o < 0 else sizes[axis] - 1
        return jnp.where(position[axis] == edge, 0.0, 1.0).astype(jnp.float32)

    for copy in first:
        copy.wait_recv()
    in_x, in_y, in_z = inside(0, 1), inside(1, 1), inside(2, 1)
    strips = [(rz[1, 1] * in_z, ryz[1, 1, 1] * (in_y * in_z)),
              (rz[2, 1] * (in_x * in_z), ryz[2, 1, 1] * (in_x * in_y * in_z))]
    for f in range(4):
        for p in range(BX + 1):
            far = p // BX
            group = 4 * (BX * f + p % BX)
            block = rxf[f] * in_x if far else own[f, p]
            line = ryf[far, BX * f + p % BX : BX * f + p % BX + 1, :] * (in_y * in_x if far else in_y)
            line = jnp.broadcast_to(line, (8, 128))
            tm[f, p, 0:16, :] = block
            tm[f, p, 16:24, :] = line
            z16, z8 = strips[far]
            tn[f, p, 0:16, :] = jnp.where(lane16 == 127, pltpu.roll(z16, 127 - group, 1), z_next(block))
            tn[f, p, 16:24, :] = jnp.where(lane8 == 127, pltpu.roll(z8, 127 - group, 1), z_next(line))

    partial = zero
    for start in (0, 8):
        old = None
        for p in range(BX + 1):
            new = []
            for f in range(4):
                a, an = tm[f, p, start : start + 8, :], tn[f, p, start : start + 8, :]
                b, bn = tm[f, p, start + 1 : start + 9, :], tn[f, p, start + 1 : start + 9, :]
                s, sn = a + b, an + bn
                new.append([s + sn, sn - s, (b - a) + (bn - an)])
            if old is not None:
                grads = [[0.25 * g for g in central_gradients(old[c], new[c])] for c in range(3)]
                rho = (old[3][0] + new[3][0]) * 0.125
                modulus = rho * rho * rho * own[5, p - 1, start : start + 8, :]
                q = modulus * modulus * unit_of(stress_of(grads))
                q = q * q
                partial = partial + q * q
            old = new
    src1[...] = partial
    sums1, sums2 = [], []
    for n, d in enumerate(plane):
        send(src1, land1.at[n], d, (s1, r1), n, sums1)

    for copy in later:
        copy.wait_recv()
    for sx in range(3):
        for sz in range(2):
            f_xz = inside(0, sx - 1) * inside(2, 2 * sz - 1)
            strip[sx, sz, 0:4, :] = ryz[sx, 0, sz, 4:8, :] * (f_xz * inside(1, -1))
            strip[sx, sz, 4:20, :] = rz[sx, sz] * f_xz
            strip[sx, sz, 20:24, :] = ryz[sx, 1, sz, 0:4, :] * (f_xz * inside(1, 1))

    def flush(stores):
        for ref, index, value in stores:
            ref[index] = value

    upper_half = rows_of() < 4

    def unpack(f, _):
        for sx in range(3):
            fx = inside(0, sx - 1)
            stores = []
            for p in range(BX):
                q = BX * sx + p
                a, b = [own[f, p, h : h + 8, :] if sx == 1 else rx[sx // 2, f, p, h : h + 8, :] * fx for h in (0, 8)]
                a, b = pltpu.roll(a, 4, 0), pltpu.roll(b, 4, 0)
                over, under = ry[sx, 0, f, p // 2] * (fx * inside(1, -1)), ry[sx, 1, f, p // 2] * (fx * inside(1, 1))
                if p % 2:
                    over = pltpu.roll(over, 4, 0)
                else:
                    under = pltpu.roll(under, 4, 0)
                chunks = [jnp.where(upper_half, over, a), jnp.where(upper_half, a, b), jnp.where(upper_half, b, under)]
                group = 4 * (BX * f + p)
                ends = None
                for t in range(3):
                    base = GROUP * t
                    below, above = strip[sx, 0, 8 * t : 8 * t + 8, :], strip[sx, 1, 8 * t : 8 * t + 8, :]
                    value = jnp.where(lane8 < base + 12, pltpu.roll(above, lax.rem(base + 8 + 128 - group, 128), 1),
                                      pltpu.roll(below, lax.rem(base + 12 + 128 - group, 128), 1))
                    value = jnp.where(lane8 < base + 8, pltpu.roll(chunks[t], base + 8, 1), value)
                    value = jnp.where(lane8 < base + 16, value, pltpu.roll(chunks[t], base + 16, 1))
                    ends = value if ends is None else jnp.where(lane8 < base, ends, value)
                    stores.append((fld, (f, q, slice(8 * t, 8 * t + 8)), chunks[t]))
                stores.append((fld, (f, q, slice(32, 40)), ends))
            flush(stores)
        return 0

    lax.fori_loop(0, 6, unpack, 0)

    kinds = ("SS", "SD", "DS", "DD")

    def scatter(t, forces, kept, stores):
        result, keep = [], []
        for c in range(3):
            by = {}
            for i, k in enumerate(kinds):
                s, d = forces[c].get("S" + k), forces[c].get("D" + k)
                if s is None and d is None:
                    continue
                if s is None:
                    by[k] = carry_p[t, 4 * c + i] - d
                    upper = d
                elif d is None:
                    by[k] = carry_p[t, 4 * c + i] + s
                    upper = s
                else:
                    by[k] = carry_p[t, 4 * c + i] + (s - d)
                    upper = s + d
                stores.append((carry_p, (t, 4 * c + i), upper))
            rows = []
            for k in ("S", "D"):
                s, d = by[k + "S"], by.get(k + "D")
                rows.append(s + z_prev(s) if d is None else (s - d) + z_prev(s + d))
            down, r = y_prev(rows[0] + rows[1], None if kept is None else kept[c], t)
            result.append((rows[0] - rows[1]) + down)
            keep.append(r)
        return result, keep

    def clear_carry():
        for i in range(12):
            for t in range(UNITS):
                carry_p[t, i] = zero

    clear_carry()
    for t in range(UNITS):
        for c in range(3):
            for i, value in enumerate(central_transform(fld, c, 0, t)):
                carry_t[t, 4 * c + i] = value
        s, _d = y_transform(fld, 3, 0, t)
        carry_t[t, 12] = s + z_next(s)

    def stage_one(e, _):
        kept, stores = None, []
        first, shear = lame_pair()
        for t in range(UNITS):
            nodes, cells = unit_rows(t), element_rows(t)
            grads = []
            for c in range(3):
                new = central_transform(fld, c, e + 1, t)
                old = [carry_t[t, 4 * c + i] for i in range(3)]
                stores += [(carry_t, (t, 4 * c + i), value) for i, value in enumerate(new)]
                grads.append([0.25 * g for g in central_gradients(old, new)])
            s, _d = y_transform(fld, 3, e + 1, t)
            mass = s + z_next(s)
            rho = (carry_t[t, 12] + mass) * 0.125
            rho_stiff = rho * rho * fld[5, e, nodes, :]
            modulus = rho_stiff * rho
            growth = 3.0 * rho_stiff
            stress = stress_of(grads)
            unit = unit_of(stress)
            square = modulus * modulus
            q = square * unit
            q3 = q * q * q
            stores += [
                (carry_t, (t, 12), mass), (mod_e, (e, cells), modulus), (grow, (e, cells), growth),
                (lead, (e, cells), growth * (8.0 * q3 * modulus * unit)),
            ]
            sxx, syy, szz, syz, sxz, sxy = stress
            weight = q3 * square
            trace = sxx + syy + szz
            hxx, hyy, hzz = 3.0 * sxx - trace, 3.0 * syy - trace, 3.0 * szz - trace
            base = first * (hxx + hyy + hzz)
            wxx = weight * (base + 2.0 * shear * hxx)
            wyy = weight * (base + 2.0 * shear * hyy)
            wzz = weight * (base + 2.0 * shear * hzz)
            skew = weight * (6.0 * shear)
            wyz, wxz, wxy = skew * syz, skew * sxz, skew * sxy
            load, kept = scatter(t, [
                {"DSS": wxx, "SDS": wxy, "SSD": wxz},
                {"DSS": wxy, "SDS": wyy, "SSD": wyz},
                {"DSS": wxz, "SDS": wyz, "SSD": wzz},
            ], kept, stores)
            free = fld[4, e, nodes, :]
            for c in range(3):
                r = free * load[c]
                d = r * (1.0 / theta)
                stores += [(rhs, (c, e, nodes), r), (v0, (c, e, nodes), d), (fv0, (c, e, nodes), free * d)]
        flush(stores)
        return 0

    lax.fori_loop(0, NP - 1, stage_one, 0)

    def apply_sweep(ref, first_plane, last_plane, node):
        clear_carry()
        for t in range(UNITS):
            for c in range(3):
                for i, value in enumerate(full_transform(ref, c, first_plane, t)):
                    carry_t[t, 4 * c + i] = value

        def body(e, _):
            kept, stores = None, []
            for t in range(UNITS):
                modes = []
                for c in range(3):
                    new = full_transform(ref, c, e + 1, t)
                    old = [carry_t[t, 4 * c + i] for i in range(4)]
                    stores += [(carry_t, (t, 4 * c + i), value) for i, value in enumerate(new)]
                    modes.append(element_modes(old, new))
                modulus = mod_e[e, element_rows(t), :]
                forces = [{k: modulus * f for k, f in g.items()} for g in element_forces(modes)]
                applied, kept = scatter(t, forces, kept, stores)
                free = fld[4, e, unit_rows(t), :]
                for c in range(3):
                    node(c, e, unit_rows(t), free, applied[c], stores)
            flush(stores)
            return 0

        lax.fori_loop(first_plane, last_plane, body, 0)

    def node_two(c, e, rows, free, applied, stores):
        d = v0[c, e, rows, :]
        r = rhs[c, e, rows, :] - (free * applied + (1.0 - free) * d)
        new = (rho_one * rho_zero) * d + (2.0 * rho_one / delta) * r
        stores += [(rhs, (c, e, rows), r), (v1, (c, e, rows), new), (fv1, (c, e, rows), free * new)]

    apply_sweep(fv0, 1, NP - 2, node_two)

    for copy in sums1:
        copy.wait_recv()
    total = src1[...]
    for n in range(len(plane)):
        total = total + land1[n]
    src2[...] = total
    for n, d in enumerate(ring):
        send(src2, land2.at[n], d, (s2, r2), n, sums2)

    def node_three(c, e, rows, free, applied, stores):
        d = v1[c, e, rows, :]
        r = rhs[c, e, rows, :] - (free * applied + (1.0 - free) * d)
        new = (rho_two * rho_one) * d + (2.0 * rho_two / delta) * r
        stores.append((adj, (c, e, rows), v0[c, e, rows, :] + d + new))

    apply_sweep(fv1, 2, NP - 3, node_three)

    for t in range(UNITS):
        carry_p[t, 0] = zero
        for c in range(3):
            for i, value in enumerate(full_transform(adj, c, W - 1, t)):
                carry_t[t, 4 * c + i] = value
            for i, value in enumerate(full_transform(fld, c, W - 1, t)):
                carry_t[t, 12 + 4 * c + i] = value

    def stage_four(e, _):
        kept, stores = None, []
        for t in range(UNITS):
            modes = []
            for ref, base in ((fld, 12), (adj, 0)):
                group = []
                for c in range(3):
                    new = full_transform(ref, c, e + 1, t)
                    old = [carry_t[t, base + 4 * c + i] for i in range(4)]
                    stores += [(carry_t, (t, base + 4 * c + i), value) for i, value in enumerate(new)]
                    group.append(element_modes(old, new))
                modes.append(group if ref is adj else element_forces(group))
            work = None
            for f, a in zip(*modes):
                for k, value in f.items():
                    work = a[k] * value if work is None else work + a[k] * value
            g = lead[e, element_rows(t), :] - grow[e, element_rows(t), :] * work
            share = g + carry_p[t, 0]
            share = share + z_prev(share)
            down, kept = y_prev(share, kept, t)
            stores += [(carry_p, (t, 0), g), (sens, (e, element_rows(t)), share + down)]
        flush(stores)
        return 0

    lax.fori_loop(W - 1, W + BX, stage_four, 0)

    for c in range(4):
        for p in range(BX):
            main, ends = ((sens.at[W + p], sens[W + p, 24:32, :]) if c == 3 else (adj.at[c, W + p], adj[c, W + p, 32:40, :]))
            for t in range(3):
                base = GROUP * t
                value = jnp.where(lane8 < 4, pltpu.roll(ends, (128 - 16 - base) % 128, 1), main[8 * t : 8 * t + 8, :])
                merged[c, p, 8 * t : 8 * t + 8, :] = jnp.where(
                    lane8 >= 124, pltpu.roll(ends, (120 - base) % 128, 1), value
                )

    for copy in sums2:
        copy.wait_recv()
    total = src2[...]
    for n in range(len(ring)):
        total = total + land2[n]
    total = jnp.sum(jnp.sum(total, axis=0, keepdims=True), axis=1, keepdims=True)
    mean = total * (1.0 / float(BX * BY * BZ * sizes[0] * sizes[1] * sizes[2]))
    aggregate = jnp.sqrt(jnp.sqrt(jnp.sqrt(mean)))
    scale = jnp.broadcast_to(aggregate / (8.0 * mean), (8, 128))
    share = scale * 0.125
    for p in range(BX):
        for h in (0, 8):
            sens_out[p, h : h + 8, :] = share * merged[3, p, h + 4 : h + 12, :]
            for c in range(3):
                adj_out[c, p, h : h + 8, :] = scale * merged[c, p, h + 4 : h + 12, :]

    for copy in first + later + sums1 + sums2:
        copy.wait_send()


def hand_over(adj_in, sens_in, adj_out, sens_out, sems):
    copies = [pltpu.make_async_copy(adj_in, adj_out, sems.at[0]), pltpu.make_async_copy(sens_in, sens_out, sems.at[1])]
    for copy in copies:
        copy.start()
    for copy in copies:
        copy.wait()


def local(sizes, displacement, density, solid, material, fixed):
    plane, ring = partners(sizes)
    f32, i32 = jnp.float32, jnp.int32
    vm = pltpu.VMEM
    dma = pltpu.SemaphoreType.DMA
    node = (3, NP, ROWS, 128)
    element = (NP, 32, 128)
    tile = (8, 128)
    messages = len(HALO) + 3
    scratch = [
        vm((3, BX, BY, BZ), f32), vm((BX, BY, BZ), f32), vm((BX, BY, BZ), i32), vm((BX, BY, BZ), i32), vm((BX, BY, BZ), i32),
        vm((6, BX, BY, BZ), f32), vm((6, 2, 8, 128), f32), vm((6, 2, 8, 128), f32),
        vm((16, 128), f32), vm((16, 128), f32), vm(tile, f32), vm(tile, f32), vm((16, 128), f32),
        vm((2, 6, BX, BY, BZ), f32), vm((3, 2, 6, 2, 8, 128), f32), vm((3, 2, 16, 128), f32), vm((3, 2, 2, 8, 128), f32),
        vm((4, 16, 128), f32), vm((2, 16, 128), f32),
        vm((3, 2, 24, 128), f32), vm((4, BX + 1, 24, 128), f32), vm((4, BX + 1, 24, 128), f32),
        vm((6, NP, ROWS, 128), f32),
        vm(element, f32), vm(element, f32), vm(element, f32),
        vm(node, f32), vm(node, f32), vm(node, f32), vm(node, f32), vm(node, f32), vm(node, f32),
        vm(element, f32), vm((4, BX, 24, 128), f32),
        vm((UNITS, 24, 8, 128), f32), vm((UNITS, 12, 8, 128), f32),
        vm(tile, f32), vm((len(plane), 8, 128), f32), vm(tile, f32), vm((len(ring), 8, 128), f32),
        dma((5,)), dma((messages,)), dma((messages,)),
        dma((len(plane),)), dma((len(plane),)), dma((len(ring),)), dma((len(ring),)),
    ]
    outs = (jax.ShapeDtypeStruct((3, BX, BY, BZ), f32), jax.ShapeDtypeStruct((BX, BY, BZ), f32))
    results = pl.pallas_call(
        functools.partial(kernel, sizes),
        out_shape=outs,
        in_specs=[pl.BlockSpec(memory_space=pltpu.HBM)] * 5,
        out_specs=(pl.BlockSpec(memory_space=pltpu.VMEM), pl.BlockSpec(memory_space=pltpu.VMEM)),
        scratch_shapes=scratch,
        compiler_params=pltpu.CompilerParams(
            collective_id=0, has_side_effects=True, vmem_limit_bytes=40 * 1024 * 1024
        ),
    )(*[pltpu.with_memory_space_constraint(x, pltpu.HBM) for x in (displacement, density, solid, material, fixed)])
    return pl.pallas_call(
        hand_over,
        out_shape=outs,
        in_specs=[pl.BlockSpec(memory_space=pl.ANY)] * 2,
        out_specs=(pl.BlockSpec(memory_space=pltpu.HBM), pl.BlockSpec(memory_space=pltpu.HBM)),
        scratch_shapes=[dma((2,))],
    )(*[pltpu.with_memory_space_constraint(x, pltpu.VMEM) for x in results])


def solution(mesh):
    sizes = tuple(mesh.shape[a] for a in AXES)
    field = P(*AXES)
    vector = P(None, *AXES)
    return jax.shard_map(
        functools.partial(local, sizes),
        mesh=mesh,
        in_specs=(vector, field, field, field, field),
        out_specs=(vector, field),
        check_vma=False,
    )
```

```python
import functools
import itertools

import jax
import jax.numpy as jnp
import numpy as np
from jax import lax
from jax.experimental import pallas as pl
from jax.experimental.pallas import tpu as pltpu
from jax.sharding import PartitionSpec as P

POISSON = 0.3
VOID_FLOOR = 0.001
MODULI = (1.0, 0.7, 0.45, 0.25)
MESH = pl.DeviceIdType.MESH
AXES = ("gx", "gy", "gz")

BX, BY, BZ = 4, 16, 128
W = 4
NP = BX + 2 * W
ROWS = 48
UNITS = 4
GROUP = 24


def lame_pair():
    first = POISSON / ((1.0 + POISSON) * (1.0 - 2.0 * POISSON))
    shear = 1.0 / (2.0 * (1.0 + POISSON))
    return (first, shear)


def corner_signs():
    return [(2 * a - 1, 2 * b - 1, 2 * c - 1) for a in (0, 1) for b in (0, 1) for c in (0, 1)]


def element_table():
    first, shear = lame_pair()
    elastic = np.zeros((6, 6))
    elastic[:3, :3] = first
    for index in range(3):
        elastic[index, index] += 2.0 * shear
        elastic[index + 3, index + 3] = shear
    point = 1.0 / np.sqrt(3.0)
    matrix = np.zeros((24, 24))
    for xi in (-point, point):
        for eta in (-point, point):
            for zeta in (-point, point):
                strain = np.zeros((6, 24))
                for index, signs in enumerate(corner_signs()):
                    sa, sb, sc = signs
                    gradx = 2.0 * sa * (1 + sb * eta) * (1 + sc * zeta) / 8.0
                    grady = 2.0 * sb * (1 + sa * xi) * (1 + sc * zeta) / 8.0
                    gradz = 2.0 * sc * (1 + sa * xi) * (1 + sb * eta) / 8.0
                    strain[0, index] = gradx
                    strain[1, 8 + index] = grady
                    strain[2, 16 + index] = gradz
                    strain[3, 8 + index] = gradz
                    strain[3, 16 + index] = grady
                    strain[4, index] = gradz
                    strain[4, 16 + index] = gradx
                    strain[5, index] = grady
                    strain[5, 8 + index] = gradx
                matrix += strain.T @ elastic @ strain / 8.0
    return matrix


def chebyshev_constants():
    rowsum = float(np.max(np.sum(np.abs(element_table()), axis=1)))
    upper = max(2.0, 8.0 * max(MODULI) * rowsum)
    lower = upper / 20.0
    theta = (upper + lower) / 2.0
    delta = (upper - lower) / 2.0
    sigma = theta / delta
    rho_zero = 1.0 / sigma
    rho_one = 1.0 / (2.0 * sigma - rho_zero)
    rho_two = 1.0 / (2.0 * sigma - rho_one)
    return (theta, delta, rho_zero, rho_one, rho_two)


HALO = [d for d in itertools.product((-1, 0, 1), repeat=3) if d != (0, 0, 0)]
FIRST = [(-1, -1, -1), (0, -1, -1), (-1, 0, -1), (-1, -1, 0), (-1, 0, 0), (0, 0, -1), (0, -1, 0)]
REST = [d for d in HALO if d not in FIRST or d[2] == 0]
REST.sort(key=lambda d: (d[1] != 0 or d[2] != 0, d[0] != 0, d[2] != 0))
LATER = [d for d in HALO if d not in FIRST]


def partners(sizes):
    nx, ny, nz = sizes

    def far(d):
        return sum(min(o % n, -o % n) for o, n in zip(d, sizes))

    plane = [(a, 0, c) for a in range(nx) for c in range(nz) if (a, c) != (0, 0)]
    ring = [(0, b, 0) for b in range(1, ny)]
    return sorted(plane, key=far, reverse=True), sorted(ring, key=far, reverse=True)


ROUNDS = [
    [d for d in HALO if d[1] == 0] + [(0, 1, 0), (0, -1, 0)],
    [(2, 0, 0), (-2, 0, 0), (0, 2, 0), (0, -2, 0)],
    [(0, 4, 0), (0, -4, 0)],
]


def z_next(x):
    return pltpu.roll(x, 127, 1)


def z_prev(x):
    return pltpu.roll(x, 1, 1)


def unit_rows(t):
    return slice(8 * t, 8 * t + 8)


def put_node(stores, ref, comp, plane, t, value):
    follow = z_next(value)
    first = 32 if t == 3 else 8 * t
    for kind, x in enumerate((value + follow, follow - value)):
        stores.append((ref, (kind, comp, plane, slice(first, first + 8)), x))
        if t == 3:
            stores.append((ref, (kind, comp, plane, slice(40, 48)), pltpu.roll(x, 128 - GROUP, 1)))


def node_rows(ref, kind, comp, plane, t):
    first = 32 if t == 3 else 8 * t
    return ref[kind, comp, plane, first : first + 8, :], ref[kind, comp, plane, first + 1 : first + 9, :]


def full_transform(ref, comp, plane, t):
    s, sn = node_rows(ref, 0, comp, plane, t)
    d, dn = node_rows(ref, 1, comp, plane, t)
    return [s + sn, d + dn, sn - s, dn - d]


def central_transform(ref, comp, plane, t):
    return full_transform(ref, comp, plane, t)[:3]


def central_gradients(old, new):
    return [new[0] - old[0], old[2] + new[2], old[1] + new[1]]


def stress_of(grads):
    first, shear = lame_pair()
    exx, eyy, ezz = grads[0][0], grads[1][1], grads[2][2]
    base = first * (exx + eyy + ezz)
    sxx, syy, szz = base + 2.0 * shear * exx, base + 2.0 * shear * eyy, base + 2.0 * shear * ezz
    syz = shear * (grads[1][2] + grads[2][1])
    sxz = shear * (grads[0][2] + grads[2][0])
    sxy = shear * (grads[0][1] + grads[1][0])
    return sxx, syy, szz, syz, sxz, sxy


def unit_of(s):
    sxx, syy, szz, syz, sxz, sxy = s
    return (
        sxx * sxx + syy * syy + szz * szz - sxx * syy - syy * szz - szz * sxx
        + 3.0 * (syz * syz + sxz * sxz + sxy * sxy)
    )


def element_modes(old, new):
    ss, sd, ds, dd = zip(old, new)
    return {
        "DSS": ss[1] - ss[0], "SSD": sd[0] + sd[1], "DSD": sd[1] - sd[0], "SDS": ds[0] + ds[1],
        "DDS": ds[1] - ds[0], "SDD": dd[0] + dd[1], "DDD": dd[1] - dd[0],
    }


def element_forces(modes, modulus):
    first, shear = lame_pair()
    u, v, w = modes
    exx, eyy, ezz = u["DSS"], v["SDS"], w["SSD"]
    normal, direct, slide = modulus * (first / 16.0), modulus * (shear / 8.0), modulus * (shear / 16.0)
    base = normal * (exx + eyy + ezz)
    sxx, syy, szz = base + direct * exx, base + direct * eyy, base + direct * ezz
    syz = slide * (v["SSD"] + w["SDS"])
    sxz = slide * (u["SSD"] + w["DSS"])
    sxy = slide * (u["SDS"] + v["DSS"])
    own, cross = modulus * ((first + 3.0 * shear) / 48.0), modulus * (first / 48.0)
    twist, cube = modulus * (shear / 48.0), modulus * ((first + 4.0 * shear) / 144.0)

    def pair(a, b):
        return own * a + cross * b, cross * a + own * b

    u_xy, w_yz = pair(u["DDS"], w["SDD"])
    u_xz, v_yz = pair(u["DSD"], v["SDD"])
    v_xy, w_xz = pair(v["DDS"], w["DSD"])
    every = u["SDD"] + v["DSD"] + w["DDS"]
    return [
        {"DSS": sxx, "SDS": sxy, "SSD": sxz, "DDS": u_xy, "DSD": u_xz,
         "SDD": twist * (every + u["SDD"]), "DDD": cube * u["DDD"]},
        {"DSS": sxy, "SDS": syy, "SSD": syz, "DDS": v_xy, "SDD": v_yz,
         "DSD": twist * (every + v["DSD"]), "DDD": cube * v["DDD"]},
        {"DSS": sxz, "SDS": syz, "SSD": szz, "SDD": w_yz, "DSD": w_xz,
         "DDS": twist * (every + w["DDS"]), "DDD": cube * w["DDD"]},
    ]


def put_shifted(ref, index, t, value):
    if t < 3:
        ref[index, 8 * t + 1 : 8 * t + 9, :] = value
    else:
        ref[index, 33:41, :] = value
        ref[index, 25:33, :] = pltpu.roll(value, GROUP, 1)


def get_shifted(ref, index, t):
    first = 32 if t == 3 else 8 * t
    return ref[index, first : first + 8, :]


def kernel(sizes, disp_in, dens_in, solid_in, mat_in, fixed_in, adj_out, sens_out,
           disp_v, dens_v, solid_v, mat_v, fixed_v, own, ylow, yhigh, zlow, zhigh, zlow_y, zhigh_y, yfirst,
           rx, ry, rz, ryz, rxf, ryf, strip, tm, tn, rows, fld, raw, mod_e, grow, lead, rhs, v0, fv0, v1, fv1, adj, fadj, sens,
           merged, shifted,
           carry_t, carry_p, src1, land1, src2, land2, in_sem, send_sem, recv_sem, s1, r1, s2, r2, known):
    position = [lax.axis_index(a) for a in AXES]

    def at(d):
        return tuple(lax.rem(p + (o % n), n) if o % n else p for p, o, n in zip(position, d, sizes))

    plane, ring = partners(sizes)
    theta, delta, rho_zero, rho_one, rho_two = chebyshev_constants()

    loads = [
        pltpu.make_async_copy(src, dst, in_sem.at[n])
        for n, (src, dst) in enumerate(
            ((disp_in, disp_v), (fixed_in, fixed_v), (dens_in, dens_v), (mat_in, mat_v), (solid_in, solid_v))
        )
    ]
    for copy in loads:
        copy.start()
    barrier = pltpu.get_barrier_semaphore()
    greeted = LATER + FIRST
    for d in greeted:
        pl.semaphore_signal(barrier, inc=1, device_id=at(d), device_id_type=MESH)
    for copy in loads:
        copy.wait()

    free = 1.0 - fixed_v[...].astype(jnp.float32)
    own[4] = free
    own[3] = dens_v[...]
    for c in range(3):
        own[c] = disp_v[c] * free
    material = mat_v[...]
    scale_class = jnp.zeros(material.shape, jnp.float32)
    for index in range(4):
        scale_class = scale_class + jnp.where(material == index, MODULI[index], 0.0).astype(jnp.float32)
    own[5] = scale_class * (VOID_FLOOR + (1.0 - VOID_FLOOR) * solid_v[...].astype(jnp.float32))

    lane16 = lax.broadcasted_iota(jnp.int32, (16, 128), 1)
    lane8 = lax.broadcasted_iota(jnp.int32, (8, 128), 1)

    def pack_lanes(first_lane, offset, ref, ref_y):
        packed = jnp.zeros((16, 128), jnp.float32)
        for f in range(6):
            for p in range(BX):
                place = 4 * (BX * f + p) + offset
                shift = (place - first_lane) % 128
                block = own[f, p]
                packed = jnp.where(lane16 < place, packed, pltpu.roll(block, shift, 1) if shift else block)
        ref[...] = packed
        ref_y[0:4, :] = packed[0:4]
        ref_y[4:8, :] = packed[12:16]

    pack_lanes(0, 0, zlow, zlow_y)
    for f in range(4):
        for p in range(BX):
            yfirst[BX * f + p : BX * f + p + 1, :] = own[f, p, 0:1, :]

    pack_lanes(124, 4, zhigh, zhigh_y)
    for f in range(6):
        for p in range(BX):
            half = 4 * (p % 2)
            ylow[f, p // 2, half : half + 4, :] = own[f, p, 0:4, :]
            yhigh[f, p // 2, half : half + 4, :] = own[f, p, 12:16, :]
    pl.semaphore_wait(barrier, len(greeted))

    def send(src, dst, d, sems, n, group):
        copy = pltpu.make_async_remote_copy(
            src_ref=src, dst_ref=dst, send_sem=sems[0].at[n], recv_sem=sems[1].at[n],
            device_id=at(d), device_id_type=MESH,
        )
        copy.start()
        group.append(copy)

    halo_sems = (send_sem, recv_sem)
    first, later = [], []
    for n, (dx, dy, dz) in enumerate(FIRST):
        sx = 1 - dx
        if dz:
            src, dst = (zlow_y, ryz.at[sx, 1, 1]) if dy else (zlow, rz.at[sx, 1])
        else:
            src, dst = (yfirst, ryf.at[sx - 1]) if dy else (own.at[pl.ds(0, 4), 0], rxf)
        send(src, dst, (dx, dy, dz), halo_sems, n, first)

    def tell(n):
        for d in ROUNDS[n]:
            pl.semaphore_signal(known.at[n], inc=1, device_id=at(d), device_id_type=MESH)

    def learn(n):
        pl.semaphore_wait(known.at[n], len(ROUNDS[n]))

    tell(0)
    later_own = []
    for n, (dx, dy, dz) in enumerate(REST):
        sx, sy, sz = 1 - dx, (1 - dy) // 2, (1 - dz) // 2
        if dz == 0 and dy == 0:
            src, dst = own, rx.at[sx // 2]
        elif dz == 0:
            src, dst = (yhigh if dy > 0 else ylow), ry.at[sx, sy]
        elif dy == 0:
            src, dst = (zhigh if dz > 0 else zlow), rz.at[sx, sz]
        else:
            src, dst = (zhigh_y if dz > 0 else zlow_y), ryz.at[sx, sy, sz]
        send(src, dst, (dx, dy, dz), halo_sems, len(FIRST) + n, later if dx else later_own)
    learn(0)
    tell(1)

    zero = jnp.zeros((8, 128), jnp.float32)

    def clear(p, _):
        for kind in range(2):
            for c in range(4):
                fld[kind, c, p, 24:32, :] = zero
            for c in range(3):
                fv0[kind, c, p, 24:32, :] = zero
                fv1[kind, c, p, 24:32, :] = zero
                fadj[kind, c, p, 24:32, :] = zero
        return 0

    for i in range(6):
        shifted[i, 0:8, :] = zero
    lax.fori_loop(0, NP, clear, 0)

    def inside(axis, o):
        if o == 0:
            return 1.0
        edge = 0 if o < 0 else sizes[axis] - 1
        return jnp.where(position[axis] == edge, 0.0, 1.0).astype(jnp.float32)

    for copy in first:
        copy.wait_recv()
    in_x, in_y, in_z = inside(0, 1), inside(1, 1), inside(2, 1)
    strips = [(rz[1, 1] * in_z, ryz[1, 1, 1] * (in_y * in_z)),
              (rz[2, 1] * (in_x * in_z), ryz[2, 1, 1] * (in_x * in_y * in_z))]
    for f in range(4):
        for p in range(BX + 1):
            far = p // BX
            group = 4 * (BX * f + p % BX)
            block = rxf[f] * in_x if far else own[f, p]
            line = ryf[far, BX * f + p % BX : BX * f + p % BX + 1, :] * (in_y * in_x if far else in_y)
            line = jnp.broadcast_to(line, (8, 128))
            tm[f, p, 0:16, :] = block
            tm[f, p, 16:24, :] = line
            z16, z8 = strips[far]
            tn[f, p, 0:16, :] = jnp.where(lane16 == 127, pltpu.roll(z16, 127 - group, 1), z_next(block))
            tn[f, p, 16:24, :] = jnp.where(lane8 == 127, pltpu.roll(z8, 127 - group, 1), z_next(line))

    partial = zero
    for start in (0, 8):
        old = None
        for p in range(BX + 1):
            new = []
            for f in range(4):
                a, an = tm[f, p, start : start + 8, :], tn[f, p, start : start + 8, :]
                b, bn = tm[f, p, start + 1 : start + 9, :], tn[f, p, start + 1 : start + 9, :]
                s, sn = a + b, an + bn
                new.append([s + sn, sn - s, (b - a) + (bn - an)])
            if old is not None:
                grads = [[0.25 * g for g in central_gradients(old[c], new[c])] for c in range(3)]
                rho = (old[3][0] + new[3][0]) * 0.125
                modulus = rho * rho * rho * own[5, p - 1, start : start + 8, :]
                q = modulus * modulus * unit_of(stress_of(grads))
                q = q * q
                partial = partial + q * q
            old = new
    src1[...] = partial
    sums1, sums2 = [], []
    learn(1)
    tell(2)
    for n, d in enumerate(plane):
        send(src1, land1.at[n], d, (s1, r1), n, sums1)

    lane24 = lax.broadcasted_iota(jnp.int32, (24, 128), 1)
    even_half = lane24 % 8 < 4
    def merge_strips(sx):
        sides = []
        for sz in range(2):
            f_xz = inside(0, sx - 1) * inside(2, 2 * sz - 1)
            strip[sx, sz, 0:4, :] = ryz[sx, 0, sz, 4:8, :] * (f_xz * inside(1, -1))
            strip[sx, sz, 4:20, :] = rz[sx, sz] * f_xz
            strip[sx, sz, 20:24, :] = ryz[sx, 1, sz, 0:4, :] * (f_xz * inside(1, 1))
            sides.append(strip[sx, sz])
        below, above = sides
        strip[sx, 0] = jnp.where(even_half, above, below)
        strip[sx, 1] = jnp.where(even_half, below, above)

    def flush(stores):
        for ref, index, value in stores:
            ref[index] = value

    def unpack(f, is_raw, parts):
        for sx in parts:
            fx = inside(0, sx - 1)
            for p in range(BX):
                q = BX * sx + p
                half = 4 * (p % 2)
                rows[q, 4:20, :] = own[f, p] if sx == 1 else rx[sx // 2, f, p] * fx
                rows[q, 0:4, :] = ry[sx, 0, f, p // 2, half : half + 4, :] * (fx * inside(1, -1))
                rows[q, 20:24, :] = ry[sx, 1, f, p // 2, half : half + 4, :] * (fx * inside(1, 1))
        for sx in parts:
            stores = []
            for p in range(BX):
                q = BX * sx + p
                group = 4 * (BX * f + p)
                units, ends = [], None
                for t in range(3):
                    base = GROUP * t
                    chunk = rows[q, 8 * t : 8 * t + 8, :]
                    outer = strip[sx, p % 2, 8 * t : 8 * t + 8, :]
                    value = jnp.where(lane8 < base + 16, pltpu.roll(outer, lax.rem(base + 8 + 128 - group, 128), 1),
                                      pltpu.roll(chunk, base + 16, 1))
                    value = jnp.where(lane8 < base + 8, pltpu.roll(chunk, base + 8, 1), value)
                    ends = value if ends is None else jnp.where(lane8 < base, ends, value)
                    units.append(chunk)
                units.append(ends)
                for t, value in enumerate(units):
                    if is_raw:
                        stores.append((raw, (f - 4, q, unit_rows(t)), value))
                    else:
                        put_node(stores, fld, f, q, t, value)
            flush(stores)

    def unpack_parts(copies, *parts):
        for copy in copies:
            copy.wait_recv()
        for sx in parts:
            merge_strips(sx)

        def nodes(f, _):
            unpack(f, False, parts)
            return 0

        def elements(f, _):
            unpack(f, True, parts)
            return 0

        lax.fori_loop(0, 4, nodes, 0)
        lax.fori_loop(4, 6, elements, 0)

    unpack_parts(later_own, 1)

    kinds = ("SS", "SD", "DS", "DD")

    def x_scatter(t, forces, stores):
        result = []
        for c in range(3):
            by = {}
            for i, k in enumerate(kinds):
                s, d = forces[c].get("S" + k), forces[c].get("D" + k)
                if s is None and d is None:
                    continue
                if s is None:
                    by[k] = carry_p[t, 4 * c + i] - d
                    upper = d
                elif d is None:
                    by[k] = carry_p[t, 4 * c + i] + s
                    upper = s
                else:
                    by[k] = carry_p[t, 4 * c + i] + (s - d)
                    upper = s + d
                stores.append((carry_p, (t, 4 * c + i), upper))
            result.append(by)
        return result

    def yz_scatter(shares):
        lower = []
        for t, group in enumerate(shares):
            for c, by in enumerate(group):
                for i, k in enumerate("SD"):
                    s, d = by["S" + k], by.get("D" + k)
                    lower.append(s if d is None else s - d)
                    put_shifted(shifted, 2 * c + i, t, s if d is None else s + d)
        result = []
        for t, group in enumerate(shares):
            values = []
            for c in range(len(group)):
                s, d = [lower[6 * t + 2 * c + i] + get_shifted(shifted, 2 * c + i, t) for i in range(2)]
                values.append((s - d) + z_prev(s + d))
            result.append(values)
        return result

    def clear_carry():
        for i in range(12):
            for t in range(UNITS):
                carry_p[t, i] = zero

    def start_one(p):
        clear_carry()
        for t in range(UNITS):
            for c in range(3):
                for i, value in enumerate(central_transform(fld, c, p, t)):
                    carry_t[t, 4 * c + i] = value
            s, sn = node_rows(fld, 0, 3, p, t)
            carry_t[t, 12] = s + sn

    def stage_one(e, _):
        stores, shares = [], []
        first, shear = lame_pair()
        for t in range(UNITS):
            cells = unit_rows(t)
            grads = []
            for c in range(3):
                new = central_transform(fld, c, e + 1, t)
                old = [carry_t[t, 4 * c + i] for i in range(3)]
                stores += [(carry_t, (t, 4 * c + i), value) for i, value in enumerate(new)]
                grads.append([0.25 * g for g in central_gradients(old, new)])
            s, sn = node_rows(fld, 0, 3, e + 1, t)
            mass = s + sn
            rho = (carry_t[t, 12] + mass) * 0.125
            rho_stiff = rho * rho * raw[1, e, cells, :]
            modulus = rho_stiff * rho
            growth = 3.0 * rho_stiff
            stress = stress_of(grads)
            unit = unit_of(stress)
            square = modulus * modulus
            q = square * unit
            q3 = q * q * q
            stores += [
                (carry_t, (t, 12), mass), (mod_e, (e, cells), modulus), (grow, (e, cells), growth),
                (lead, (e, cells), growth * (8.0 * q3 * modulus * unit)),
            ]
            sxx, syy, szz, syz, sxz, sxy = stress
            weight = q3 * square
            trace = sxx + syy + szz
            hxx, hyy, hzz = 3.0 * sxx - trace, 3.0 * syy - trace, 3.0 * szz - trace
            base = first * (hxx + hyy + hzz)
            wxx = weight * (base + 2.0 * shear * hxx)
            wyy = weight * (base + 2.0 * shear * hyy)
            wzz = weight * (base + 2.0 * shear * hzz)
            skew = weight * (6.0 * shear)
            wyz, wxz, wxy = skew * syz, skew * sxz, skew * sxy
            shares.append(x_scatter(t, [
                {"DSS": wxx, "SDS": wxy, "SSD": wxz},
                {"DSS": wxy, "SDS": wyy, "SSD": wyz},
                {"DSS": wxz, "SDS": wyz, "SSD": wzz},
            ], stores))
        for t, load in enumerate(yz_scatter(shares)):
            cells = unit_rows(t)
            free = raw[0, e, cells, :]
            for c in range(3):
                r = free * load[c]
                d = r * (1.0 / theta)
                stores += [(rhs, (c, e, cells), r), (v0, (c, e, cells), d)]
                put_node(stores, fv0, c, e, t, free * d)
        flush(stores)
        return 0

    start_one(W)
    lax.fori_loop(W, W + BX - 1, stage_one, 0)
    unpack_parts(later, 0, 2)
    lax.fori_loop(W + BX - 1, NP - 1, stage_one, 0)
    start_one(0)
    lax.fori_loop(0, W + 1, stage_one, 0)

    def apply_sweep(ref, first_plane, last_plane, node):
        clear_carry()
        for t in range(UNITS):
            for c in range(3):
                for i, value in enumerate(full_transform(ref, c, first_plane, t)):
                    carry_t[t, 4 * c + i] = value

        def body(e, _):
            stores, shares = [], []
            for t in range(UNITS):
                modes = []
                for c in range(3):
                    new = full_transform(ref, c, e + 1, t)
                    old = [carry_t[t, 4 * c + i] for i in range(4)]
                    stores += [(carry_t, (t, 4 * c + i), value) for i, value in enumerate(new)]
                    modes.append(element_modes(old, new))
                forces = element_forces(modes, mod_e[e, unit_rows(t), :])
                shares.append(x_scatter(t, forces, stores))
            for t, applied in enumerate(yz_scatter(shares)):
                free = raw[0, e, unit_rows(t), :]
                for c in range(3):
                    node(c, e, t, free, applied[c], stores)
            flush(stores)
            return 0

        lax.fori_loop(first_plane, last_plane, body, 0)

    def node_two(c, e, t, free, applied, stores):
        cells = unit_rows(t)
        d = v0[c, e, cells, :]
        r = rhs[c, e, cells, :] - (free * applied + (1.0 - free) * d)
        new = (rho_one * rho_zero) * d + (2.0 * rho_one / delta) * r
        stores += [(rhs, (c, e, cells), r), (v1, (c, e, cells), new)]
        put_node(stores, fv1, c, e, t, free * new)

    for copy in sums1:
        copy.wait_recv()
    total = src1[...]
    for n in range(len(plane)):
        total = total + land1[n]
    src2[...] = total
    learn(2)
    for n, d in enumerate(ring):
        send(src2, land2.at[n], d, (s2, r2), n, sums2)

    apply_sweep(fv0, 1, NP - 2, node_two)

    def node_three(c, e, t, free, applied, stores):
        cells = unit_rows(t)
        d = v1[c, e, cells, :]
        r = rhs[c, e, cells, :] - (free * applied + (1.0 - free) * d)
        new = (rho_two * rho_one) * d + (2.0 * rho_two / delta) * r
        value = v0[c, e, cells, :] + d + new
        stores.append((adj, (c, e, cells), value))
        put_node(stores, fadj, c, e, t, value)

    apply_sweep(fv1, 2, NP - 3, node_three)

    for t in range(UNITS):
        carry_p[t, 0] = zero
        for c in range(3):
            for i, value in enumerate(full_transform(fadj, c, W - 1, t)):
                carry_t[t, 4 * c + i] = value
            for i, value in enumerate(full_transform(fld, c, W - 1, t)):
                carry_t[t, 12 + 4 * c + i] = value

    def stage_four(e, _):
        stores, shares = [], []
        for t in range(UNITS):
            modes = []
            for ref, base in ((fld, 12), (fadj, 0)):
                group = []
                for c in range(3):
                    new = full_transform(ref, c, e + 1, t)
                    old = [carry_t[t, base + 4 * c + i] for i in range(4)]
                    stores += [(carry_t, (t, base + 4 * c + i), value) for i, value in enumerate(new)]
                    group.append(element_modes(old, new))
                modes.append(group if base == 0 else element_forces(group, 1.0))
            work = None
            for f, a in zip(*modes):
                for k, value in f.items():
                    work = a[k] * value if work is None else work + a[k] * value
            g = lead[e, unit_rows(t), :] - grow[e, unit_rows(t), :] * work
            share = g + carry_p[t, 0]
            stores.append((carry_p, (t, 0), g))
            put_shifted(shifted, 0, t, share)
            shares.append(share)
        for t, share in enumerate(shares):
            share = share + get_shifted(shifted, 0, t)
            stores.append((sens, (e, unit_rows(t)), share + z_prev(share)))
        flush(stores)
        return 0

    lax.fori_loop(W - 1, W + BX, stage_four, 0)

    for c in range(4):
        for p in range(BX):
            main, ends = ((sens.at[W + p], sens[W + p, 24:32, :]) if c == 3 else (adj.at[c, W + p], adj[c, W + p, 24:32, :]))
            for t in range(3):
                base = GROUP * t
                value = jnp.where(lane8 < 4, pltpu.roll(ends, (128 - 16 - base) % 128, 1), main[8 * t : 8 * t + 8, :])
                merged[c, p, 8 * t : 8 * t + 8, :] = jnp.where(
                    lane8 >= 124, pltpu.roll(ends, (120 - base) % 128, 1), value
                )

    for copy in first + later_own + later + sums1:
        copy.wait_send()
    for copy in sums2:
        copy.wait_recv()
    total = src2[...]
    for n in range(len(ring)):
        total = total + land2[n]
    total = jnp.sum(jnp.sum(total, axis=0, keepdims=True), axis=1, keepdims=True)
    mean = total * (1.0 / float(BX * BY * BZ * sizes[0] * sizes[1] * sizes[2]))
    aggregate = jnp.sqrt(jnp.sqrt(jnp.sqrt(mean)))
    scale = jnp.broadcast_to(aggregate / (8.0 * mean), (8, 128))
    share = scale * 0.125
    for p in range(BX):
        for h in (0, 8):
            sens_out[p, h : h + 8, :] = share * merged[3, p, h + 4 : h + 12, :]
            for c in range(3):
                adj_out[c, p, h : h + 8, :] = scale * merged[c, p, h + 4 : h + 12, :]

    for copy in sums2:
        copy.wait_send()


def hand_over(adj_in, sens_in, adj_out, sens_out, sems):
    copies = [pltpu.make_async_copy(adj_in, adj_out, sems.at[0]), pltpu.make_async_copy(sens_in, sens_out, sems.at[1])]
    for copy in copies:
        copy.start()
    for copy in copies:
        copy.wait()


def local(sizes, displacement, density, solid, material, fixed):
    plane, ring = partners(sizes)
    f32, i32 = jnp.float32, jnp.int32
    vm = pltpu.VMEM
    dma = pltpu.SemaphoreType.DMA
    node, paired = (3, NP, 32, 128), (2, 3, NP, ROWS, 128)
    element = (NP, 32, 128)
    tile = (8, 128)
    messages = len(HALO) + 3
    scratch = [
        vm((3, BX, BY, BZ), f32), vm((BX, BY, BZ), f32), vm((BX, BY, BZ), i32), vm((BX, BY, BZ), i32), vm((BX, BY, BZ), i32),
        vm((6, BX, BY, BZ), f32), vm((6, 2, 8, 128), f32), vm((6, 2, 8, 128), f32),
        vm((16, 128), f32), vm((16, 128), f32), vm(tile, f32), vm(tile, f32), vm((16, 128), f32),
        vm((2, 6, BX, BY, BZ), f32), vm((3, 2, 6, 2, 8, 128), f32), vm((3, 2, 16, 128), f32), vm((3, 2, 2, 8, 128), f32),
        vm((4, 16, 128), f32), vm((2, 16, 128), f32),
        vm((3, 2, 24, 128), f32), vm((4, BX + 1, 24, 128), f32), vm((4, BX + 1, 24, 128), f32),
        vm((NP, 24, 128), f32), vm((2, 4, NP, ROWS, 128), f32), vm((2, NP, 32, 128), f32),
        vm(element, f32), vm(element, f32), vm(element, f32),
        vm(node, f32), vm(node, f32), vm(paired, f32), vm(node, f32), vm(paired, f32), vm(node, f32), vm(paired, f32),
        vm(element, f32), vm((4, BX, 24, 128), f32), vm((6, ROWS, 128), f32),
        vm((UNITS, 24, 8, 128), f32), vm((UNITS, 12, 8, 128), f32),
        vm(tile, f32), vm((len(plane), 8, 128), f32), vm(tile, f32), vm((len(ring), 8, 128), f32),
        dma((5,)), dma((messages,)), dma((messages,)),
        dma((len(plane),)), dma((len(plane),)), dma((len(ring),)), dma((len(ring),)),
        pltpu.SemaphoreType.REGULAR((len(ROUNDS),)),
    ]
    outs = (jax.ShapeDtypeStruct((3, BX, BY, BZ), f32), jax.ShapeDtypeStruct((BX, BY, BZ), f32))
    results = pl.pallas_call(
        functools.partial(kernel, sizes),
        out_shape=outs,
        in_specs=[pl.BlockSpec(memory_space=pltpu.HBM)] * 5,
        out_specs=(pl.BlockSpec(memory_space=pltpu.VMEM), pl.BlockSpec(memory_space=pltpu.VMEM)),
        scratch_shapes=scratch,
        compiler_params=pltpu.CompilerParams(
            collective_id=0, has_side_effects=True, vmem_limit_bytes=40 * 1024 * 1024
        ),
    )(*[pltpu.with_memory_space_constraint(x, pltpu.HBM) for x in (displacement, density, solid, material, fixed)])
    return pl.pallas_call(
        hand_over,
        out_shape=outs,
        in_specs=[pl.BlockSpec(memory_space=pl.ANY)] * 2,
        out_specs=(pl.BlockSpec(memory_space=pltpu.HBM), pl.BlockSpec(memory_space=pltpu.HBM)),
        scratch_shapes=[dma((2,))],
    )(*[pltpu.with_memory_space_constraint(x, pltpu.VMEM) for x in results])


def solution(mesh):
    sizes = tuple(mesh.shape[a] for a in AXES)
    field = P(*AXES)
    vector = P(None, *AXES)
    return jax.shard_map(
        functools.partial(local, sizes),
        mesh=mesh,
        in_specs=(vector, field, field, field, field),
        out_specs=(vector, field),
        check_vma=False,
    )
```

```python
import functools
import itertools

import jax
import jax.numpy as jnp
import numpy as np
from jax import lax
from jax.experimental import pallas as pl
from jax.experimental.pallas import tpu as pltpu
from jax.sharding import PartitionSpec as P

POISSON = 0.3
VOID_FLOOR = 0.001
MODULI = (1.0, 0.7, 0.45, 0.25)
MESH = pl.DeviceIdType.MESH
AXES = ("gx", "gy", "gz")

BX, BY, BZ = 4, 16, 128
W = 4
NP = BX + 2 * W
ROWS = 56
UNITS = 4
GROUP = 24


def lame_pair():
    first = POISSON / ((1.0 + POISSON) * (1.0 - 2.0 * POISSON))
    shear = 1.0 / (2.0 * (1.0 + POISSON))
    return (first, shear)


def corner_signs():
    return [(2 * a - 1, 2 * b - 1, 2 * c - 1) for a in (0, 1) for b in (0, 1) for c in (0, 1)]


def element_table():
    first, shear = lame_pair()
    elastic = np.zeros((6, 6))
    elastic[:3, :3] = first
    for index in range(3):
        elastic[index, index] += 2.0 * shear
        elastic[index + 3, index + 3] = shear
    point = 1.0 / np.sqrt(3.0)
    matrix = np.zeros((24, 24))
    for xi in (-point, point):
        for eta in (-point, point):
            for zeta in (-point, point):
                strain = np.zeros((6, 24))
                for index, signs in enumerate(corner_signs()):
                    sa, sb, sc = signs
                    gradx = 2.0 * sa * (1 + sb * eta) * (1 + sc * zeta) / 8.0
                    grady = 2.0 * sb * (1 + sa * xi) * (1 + sc * zeta) / 8.0
                    gradz = 2.0 * sc * (1 + sa * xi) * (1 + sb * eta) / 8.0
                    strain[0, index] = gradx
                    strain[1, 8 + index] = grady
                    strain[2, 16 + index] = gradz
                    strain[3, 8 + index] = gradz
                    strain[3, 16 + index] = grady
                    strain[4, index] = gradz
                    strain[4, 16 + index] = gradx
                    strain[5, index] = grady
                    strain[5, 8 + index] = gradx
                matrix += strain.T @ elastic @ strain / 8.0
    return matrix


def chebyshev_constants():
    rowsum = float(np.max(np.sum(np.abs(element_table()), axis=1)))
    upper = max(2.0, 8.0 * max(MODULI) * rowsum)
    lower = upper / 20.0
    theta = (upper + lower) / 2.0
    delta = (upper - lower) / 2.0
    sigma = theta / delta
    rho_zero = 1.0 / sigma
    rho_one = 1.0 / (2.0 * sigma - rho_zero)
    rho_two = 1.0 / (2.0 * sigma - rho_one)
    return (theta, delta, rho_zero, rho_one, rho_two)


HALO = [d for d in itertools.product((-1, 0, 1), repeat=3) if d != (0, 0, 0)]
FIRST = [(-1, -1, -1), (0, -1, -1), (-1, 0, -1), (-1, -1, 0), (-1, 0, 0), (0, 0, -1), (0, -1, 0)]
REST = [d for d in HALO if d not in FIRST or d[2] == 0]
REST.sort(key=lambda d: (d[1] != 0 or d[2] != 0, d[0] != 0, d[2] != 0))
LATER = [d for d in HALO if d not in FIRST]


def partners(sizes):
    nx, ny, nz = sizes

    def far(d):
        return sum(min(o % n, -o % n) for o, n in zip(d, sizes))

    plane = [(a, 0, c) for a in range(nx) for c in range(nz) if (a, c) != (0, 0)]
    ring = [(0, b, 0) for b in range(1, ny)]
    return sorted(plane, key=far, reverse=True), sorted(ring, key=far, reverse=True)


ROUNDS = [
    [d for d in HALO if d[1] == 0] + [(0, 1, 0), (0, -1, 0)],
    [(2, 0, 0), (-2, 0, 0), (0, 2, 0), (0, -2, 0)],
    [(0, 4, 0), (0, -4, 0)],
]


def z_next(x):
    return pltpu.roll(x, 127, 1)


def z_prev(x):
    return pltpu.roll(x, 1, 1)


def unit_rows(t):
    return slice(8 * t, 8 * t + 8)


def put_node(stores, ref, comp, plane, t, value):
    follow = z_next(value)
    first = 32 if t == 3 else 8 * t
    for kind, x in enumerate((value + follow, follow - value)):
        stores.append((ref, (plane, kind, comp, slice(first, first + 8)), x))
        if t == 3:
            stores.append((ref, (plane, kind, comp, slice(40, 48)), pltpu.roll(x, 128 - GROUP, 1)))


def node_rows(ref, kind, comp, plane, t):
    first = 32 if t == 3 else 8 * t
    return ref[plane, kind, comp, first : first + 8, :], ref[plane, kind, comp, first + 1 : first + 9, :]


def full_transform(ref, comp, plane, t):
    s, sn = node_rows(ref, 0, comp, plane, t)
    d, dn = node_rows(ref, 1, comp, plane, t)
    return [s + sn, d + dn, sn - s, dn - d]


def central_transform(ref, comp, plane, t):
    return full_transform(ref, comp, plane, t)[:3]


def central_gradients(old, new):
    return [new[0] - old[0], old[2] + new[2], old[1] + new[1]]


def stress_of(grads):
    first, shear = lame_pair()
    exx, eyy, ezz = grads[0][0], grads[1][1], grads[2][2]
    base = first * (exx + eyy + ezz)
    sxx, syy, szz = base + 2.0 * shear * exx, base + 2.0 * shear * eyy, base + 2.0 * shear * ezz
    syz = shear * (grads[1][2] + grads[2][1])
    sxz = shear * (grads[0][2] + grads[2][0])
    sxy = shear * (grads[0][1] + grads[1][0])
    return sxx, syy, szz, syz, sxz, sxy


def unit_of(s):
    sxx, syy, szz, syz, sxz, sxy = s
    return (
        sxx * sxx + syy * syy + szz * szz - sxx * syy - syy * szz - szz * sxx
        + 3.0 * (syz * syz + sxz * sxz + sxy * sxy)
    )


def element_modes(old, new):
    ss, sd, ds, dd = zip(old, new)
    return {
        "DSS": ss[1] - ss[0], "SSD": sd[0] + sd[1], "DSD": sd[1] - sd[0], "SDS": ds[0] + ds[1],
        "DDS": ds[1] - ds[0], "SDD": dd[0] + dd[1], "DDD": dd[1] - dd[0],
    }


def element_forces(modes, modulus):
    first, shear = lame_pair()
    u, v, w = modes
    exx, eyy, ezz = u["DSS"], v["SDS"], w["SSD"]
    normal, direct, slide = modulus * (first / 16.0), modulus * (shear / 8.0), modulus * (shear / 16.0)
    base = normal * (exx + eyy + ezz)
    sxx, syy, szz = base + direct * exx, base + direct * eyy, base + direct * ezz
    syz = slide * (v["SSD"] + w["SDS"])
    sxz = slide * (u["SSD"] + w["DSS"])
    sxy = slide * (u["SDS"] + v["DSS"])
    own, cross = modulus * ((first + 3.0 * shear) / 48.0), modulus * (first / 48.0)
    twist, cube = modulus * (shear / 48.0), modulus * ((first + 4.0 * shear) / 144.0)

    def pair(a, b):
        return own * a + cross * b, cross * a + own * b

    u_xy, w_yz = pair(u["DDS"], w["SDD"])
    u_xz, v_yz = pair(u["DSD"], v["SDD"])
    v_xy, w_xz = pair(v["DDS"], w["DSD"])
    every = u["SDD"] + v["DSD"] + w["DDS"]
    return [
        {"DSS": sxx, "SDS": sxy, "SSD": sxz, "DDS": u_xy, "DSD": u_xz,
         "SDD": twist * (every + u["SDD"]), "DDD": cube * u["DDD"]},
        {"DSS": sxy, "SDS": syy, "SSD": syz, "DDS": v_xy, "SDD": v_yz,
         "DSD": twist * (every + v["DSD"]), "DDD": cube * v["DDD"]},
        {"DSS": sxz, "SDS": syz, "SSD": szz, "SDD": w_yz, "DSD": w_xz,
         "DDS": twist * (every + w["DDS"]), "DDD": cube * w["DDD"]},
    ]


def put_shifted(ref, index, t, value):
    if t < 3:
        ref[index, 8 * t + 1 : 8 * t + 9, :] = value
    else:
        ref[index, 33:41, :] = value
        ref[index, 25:33, :] = pltpu.roll(value, GROUP, 1)


def get_shifted(ref, index, t):
    first = 32 if t == 3 else 8 * t
    return ref[index, first : first + 8, :]


def kernel(sizes, disp_in, dens_in, solid_in, mat_in, fixed_in, adj_out, sens_out,
           disp_v, dens_v, solid_v, mat_v, fixed_v, own, ylow, yhigh, zlow, zhigh, zlow_y, zhigh_y, yfirst,
           rx, ry, rz, ryz, rxf, ryf, strip, tm, tn, rows, fld, raw, mod_e, grow, lead, rhs, v0, fv0, v1, fv1, adj, fadj, sens,
           merged, shifted, lowers,
           carry_t, carry_p, src1, land1, src2, land2, in_sem, send_sem, recv_sem, s1, r1, s2, r2, known):
    position = [lax.axis_index(a) for a in AXES]

    def at(d):
        return tuple(lax.rem(p + (o % n), n) if o % n else p for p, o, n in zip(position, d, sizes))

    plane, ring = partners(sizes)
    theta, delta, rho_zero, rho_one, rho_two = chebyshev_constants()

    loads = [
        pltpu.make_async_copy(src, dst, in_sem.at[n])
        for n, (src, dst) in enumerate(
            ((disp_in, disp_v), (fixed_in, fixed_v), (dens_in, dens_v), (mat_in, mat_v), (solid_in, solid_v))
        )
    ]
    for copy in loads:
        copy.start()
    barrier = pltpu.get_barrier_semaphore()
    greeted = LATER + FIRST
    for d in greeted:
        pl.semaphore_signal(barrier, inc=1, device_id=at(d), device_id_type=MESH)
    for copy in loads:
        copy.wait()

    free = 1.0 - fixed_v[...].astype(jnp.float32)
    own[4] = free
    own[3] = dens_v[...]
    for c in range(3):
        own[c] = disp_v[c] * free
    material = mat_v[...]
    scale_class = jnp.zeros(material.shape, jnp.float32)
    for index in range(4):
        scale_class = scale_class + jnp.where(material == index, MODULI[index], 0.0).astype(jnp.float32)
    own[5] = scale_class * (VOID_FLOOR + (1.0 - VOID_FLOOR) * solid_v[...].astype(jnp.float32))

    lane16 = lax.broadcasted_iota(jnp.int32, (16, 128), 1)
    lane8 = lax.broadcasted_iota(jnp.int32, (8, 128), 1)

    def pack_lanes(first_lane, offset, ref, ref_y):
        packed = jnp.zeros((16, 128), jnp.float32)
        for f in range(6):
            for p in range(BX):
                place = 4 * (BX * f + p) + offset
                shift = (place - first_lane) % 128
                block = own[f, p]
                packed = jnp.where(lane16 < place, packed, pltpu.roll(block, shift, 1) if shift else block)
        ref[...] = packed
        ref_y[0:4, :] = packed[0:4]
        ref_y[4:8, :] = packed[12:16]

    pack_lanes(0, 0, zlow, zlow_y)
    for f in range(4):
        for p in range(BX):
            yfirst[BX * f + p : BX * f + p + 1, :] = own[f, p, 0:1, :]

    pack_lanes(124, 4, zhigh, zhigh_y)
    for f in range(6):
        for p in range(BX):
            half = 4 * (p % 2)
            ylow[f, p // 2, half : half + 4, :] = own[f, p, 0:4, :]
            yhigh[f, p // 2, half : half + 4, :] = own[f, p, 12:16, :]
    pl.semaphore_wait(barrier, len(greeted))

    def send(src, dst, d, sems, n, group):
        copy = pltpu.make_async_remote_copy(
            src_ref=src, dst_ref=dst, send_sem=sems[0].at[n], recv_sem=sems[1].at[n],
            device_id=at(d), device_id_type=MESH,
        )
        copy.start()
        group.append(copy)

    halo_sems = (send_sem, recv_sem)
    first, later = [], []
    for n, (dx, dy, dz) in enumerate(FIRST):
        sx = 1 - dx
        if dz:
            src, dst = (zlow_y, ryz.at[sx, 1, 1]) if dy else (zlow, rz.at[sx, 1])
        else:
            src, dst = (yfirst, ryf.at[sx - 1]) if dy else (own.at[pl.ds(0, 4), 0], rxf)
        send(src, dst, (dx, dy, dz), halo_sems, n, first)

    def tell(n):
        for d in ROUNDS[n]:
            pl.semaphore_signal(known.at[n], inc=1, device_id=at(d), device_id_type=MESH)

    def learn(n):
        pl.semaphore_wait(known.at[n], len(ROUNDS[n]))

    later_own = []
    for n, (dx, dy, dz) in enumerate(REST):
        sx, sy, sz = 1 - dx, (1 - dy) // 2, (1 - dz) // 2
        if dz == 0 and dy == 0:
            src, dst = own, rx.at[sx // 2]
        elif dz == 0:
            src, dst = (yhigh if dy > 0 else ylow), ry.at[sx, sy]
        elif dy == 0:
            src, dst = (zhigh if dz > 0 else zlow), rz.at[sx, sz]
        else:
            src, dst = (zhigh_y if dz > 0 else zlow_y), ryz.at[sx, sy, sz]
        send(src, dst, (dx, dy, dz), halo_sems, len(FIRST) + n, later if dx else later_own)
        if n == 7:
            tell(0)
    learn(0)
    tell(1)

    zero = jnp.zeros((8, 128), jnp.float32)

    def clear(p, _):
        for kind in range(2):
            for c in range(4):
                fld[p, kind, c, 24:32, :] = zero
            for c in range(3):
                fv0[p, kind, c, 24:32, :] = zero
                fv1[p, kind, c, 24:32, :] = zero
                fadj[p, kind, c, 24:32, :] = zero
        return 0

    for i in range(6):
        shifted[i, 0:8, :] = zero
    for i in range(24):
        lowers[i] = zero
        shifted[i % 6, 8 + 8 * (i // 6) : 16 + 8 * (i // 6), :] = zero
    lax.fori_loop(0, NP, clear, 0)

    def inside(axis, o):
        if o == 0:
            return 1.0
        edge = 0 if o < 0 else sizes[axis] - 1
        return jnp.where(position[axis] == edge, 0.0, 1.0).astype(jnp.float32)

    for copy in first:
        copy.wait_recv()
    in_x, in_y, in_z = inside(0, 1), inside(1, 1), inside(2, 1)
    strips = [(rz[1, 1] * in_z, ryz[1, 1, 1] * (in_y * in_z)),
              (rz[2, 1] * (in_x * in_z), ryz[2, 1, 1] * (in_x * in_y * in_z))]
    for f in range(4):
        for p in range(BX + 1):
            far = p // BX
            group = 4 * (BX * f + p % BX)
            block = rxf[f] * in_x if far else own[f, p]
            line = ryf[far, BX * f + p % BX : BX * f + p % BX + 1, :] * (in_y * in_x if far else in_y)
            line = jnp.broadcast_to(line, (8, 128))
            tm[f, p, 0:16, :] = block
            tm[f, p, 16:24, :] = line
            z16, z8 = strips[far]
            tn[f, p, 0:16, :] = jnp.where(lane16 == 127, pltpu.roll(z16, 127 - group, 1), z_next(block))
            tn[f, p, 16:24, :] = jnp.where(lane8 == 127, pltpu.roll(z8, 127 - group, 1), z_next(line))

    partial = zero
    for start in (0, 8):
        old = None
        for p in range(BX + 1):
            new = []
            for f in range(4):
                a, an = tm[f, p, start : start + 8, :], tn[f, p, start : start + 8, :]
                b, bn = tm[f, p, start + 1 : start + 9, :], tn[f, p, start + 1 : start + 9, :]
                s, sn = a + b, an + bn
                new.append([s + sn, sn - s, (b - a) + (bn - an)])
            if old is not None:
                grads = [[0.25 * g for g in central_gradients(old[c], new[c])] for c in range(3)]
                rho = (old[3][0] + new[3][0]) * 0.125
                modulus = rho * rho * rho * own[5, p - 1, start : start + 8, :]
                q = modulus * modulus * unit_of(stress_of(grads))
                q = q * q
                partial = partial + q * q
            old = new
    src1[...] = partial
    sums1, sums2 = [], []
    learn(1)
    tell(2)
    for n, d in enumerate(plane):
        send(src1, land1.at[n], d, (s1, r1), n, sums1)

    lane24 = lax.broadcasted_iota(jnp.int32, (24, 128), 1)
    even_half = lane24 % 8 < 4
    def merge_strips(sx):
        sides = []
        for sz in range(2):
            f_xz = inside(0, sx - 1) * inside(2, 2 * sz - 1)
            strip[sx, sz, 0:4, :] = ryz[sx, 0, sz, 4:8, :] * (f_xz * inside(1, -1))
            strip[sx, sz, 4:20, :] = rz[sx, sz] * f_xz
            strip[sx, sz, 20:24, :] = ryz[sx, 1, sz, 0:4, :] * (f_xz * inside(1, 1))
            sides.append(strip[sx, sz])
        below, above = sides
        strip[sx, 0] = jnp.where(even_half, above, below)
        strip[sx, 1] = jnp.where(even_half, below, above)

    def flush(stores):
        for ref, index, value in stores:
            ref[index] = value

    def unpack(f, is_raw, parts):
        for sx in parts:
            fx = inside(0, sx - 1)
            for p in range(BX):
                q = BX * sx + p
                half = 4 * (p % 2)
                rows[q, 4:20, :] = own[f, p] if sx == 1 else rx[sx // 2, f, p] * fx
                rows[q, 0:4, :] = ry[sx, 0, f, p // 2, half : half + 4, :] * (fx * inside(1, -1))
                rows[q, 20:24, :] = ry[sx, 1, f, p // 2, half : half + 4, :] * (fx * inside(1, 1))
        for sx in parts:
            stores = []
            for p in range(BX):
                q = BX * sx + p
                group = 4 * (BX * f + p)
                units, ends = [], None
                for t in range(3):
                    base = GROUP * t
                    chunk = rows[q, 8 * t : 8 * t + 8, :]
                    outer = strip[sx, p % 2, 8 * t : 8 * t + 8, :]
                    value = jnp.where(lane8 < base + 16, pltpu.roll(outer, lax.rem(base + 8 + 128 - group, 128), 1),
                                      pltpu.roll(chunk, base + 16, 1))
                    value = jnp.where(lane8 < base + 8, pltpu.roll(chunk, base + 8, 1), value)
                    ends = value if ends is None else jnp.where(lane8 < base, ends, value)
                    units.append(chunk)
                units.append(ends)
                for t, value in enumerate(units):
                    if is_raw:
                        stores.append((raw, (q, f - 4, unit_rows(t)), value))
                    else:
                        put_node(stores, fld, f, q, t, value)
            flush(stores)

    def unpack_parts(copies, *parts):
        for copy in copies:
            copy.wait_recv()
        for sx in parts:
            merge_strips(sx)

        def nodes(f, _):
            unpack(f, False, parts)
            return 0

        def elements(f, _):
            unpack(f, True, parts)
            return 0

        lax.fori_loop(0, 4, nodes, 0)
        lax.fori_loop(4, 6, elements, 0)

    unpack_parts(later_own, 1)

    kinds = ("SS", "SD", "DS", "DD")

    def x_scatter(t, forces, stores):
        result = []
        for c in range(3):
            by = {}
            for i, k in enumerate(kinds):
                s, d = forces[c].get("S" + k), forces[c].get("D" + k)
                if s is None and d is None:
                    continue
                if s is None:
                    by[k] = carry_p[t, 4 * c + i] - d
                    upper = d
                elif d is None:
                    by[k] = carry_p[t, 4 * c + i] + s
                    upper = s
                else:
                    by[k] = carry_p[t, 4 * c + i] + (s - d)
                    upper = s + d
                stores.append((carry_p, (t, 4 * c + i), upper))
            result.append(by)
        return result

    def leave(shares, stores):
        for t, group in enumerate(shares):
            for c, by in enumerate(group):
                for i, k in enumerate("SD"):
                    s, d = by["S" + k], by.get("D" + k)
                    lower, upper = (s, s) if d is None else (s - d, s + d)
                    stores.append((lowers, 6 * t + 2 * c + i, lower))
                    index = 2 * c + i
                    if t < 3:
                        stores.append((shifted, (index, slice(8 * t + 1, 8 * t + 9)), upper))
                    else:
                        stores.append((shifted, (index, slice(33, 41)), upper))
                        stores.append((shifted, (index, slice(25, 33)), pltpu.roll(upper, GROUP, 1)))

    def take_up():
        result = []
        for t in range(UNITS):
            values = []
            for c in range(3):
                s, d = [lowers[6 * t + 2 * c + i] + get_shifted(shifted, 2 * c + i, t) for i in range(2)]
                values.append((s - d) + z_prev(s + d))
            result.append(values)
        return result

    def clear_carry():
        for i in range(12):
            for t in range(UNITS):
                carry_p[t, i] = zero

    def start_one(p):
        clear_carry()
        for t in range(UNITS):
            for c in range(3):
                for i, value in enumerate(central_transform(fld, c, p, t)):
                    carry_t[t, 4 * c + i] = value
            s, sn = node_rows(fld, 0, 3, p, t)
            carry_t[t, 12] = s + sn

    def nodes_one(e, stores):
        for t, load in enumerate(take_up()):
            cells = unit_rows(t)
            free = raw[e, 0, cells, :]
            for c in range(3):
                r = free * load[c]
                d = r * (1.0 / theta)
                stores += [(rhs, (e, c, cells), r), (v0, (e, c, cells), d)]
                put_node(stores, fv0, c, e, t, free * d)

    def stage_one(e, _):
        stores, shares = [], []
        nodes_one(jnp.maximum(e - 1, 0), stores)
        first, shear = lame_pair()
        for t in range(UNITS):
            cells = unit_rows(t)
            grads = []
            for c in range(3):
                new = central_transform(fld, c, e + 1, t)
                old = [carry_t[t, 4 * c + i] for i in range(3)]
                stores += [(carry_t, (t, 4 * c + i), value) for i, value in enumerate(new)]
                grads.append([0.25 * g for g in central_gradients(old, new)])
            s, sn = node_rows(fld, 0, 3, e + 1, t)
            mass = s + sn
            rho = (carry_t[t, 12] + mass) * 0.125
            rho_stiff = rho * rho * raw[e, 1, cells, :]
            modulus = rho_stiff * rho
            growth = 3.0 * rho_stiff
            stress = stress_of(grads)
            unit = unit_of(stress)
            square = modulus * modulus
            q = square * unit
            q3 = q * q * q
            stores += [
                (carry_t, (t, 12), mass), (mod_e, (e, cells), modulus), (grow, (e, cells), growth),
                (lead, (e, cells), growth * (8.0 * q3 * modulus * unit)),
            ]
            sxx, syy, szz, syz, sxz, sxy = stress
            weight = q3 * square
            trace = sxx + syy + szz
            hxx, hyy, hzz = 3.0 * sxx - trace, 3.0 * syy - trace, 3.0 * szz - trace
            base = first * (hxx + hyy + hzz)
            wxx = weight * (base + 2.0 * shear * hxx)
            wyy = weight * (base + 2.0 * shear * hyy)
            wzz = weight * (base + 2.0 * shear * hzz)
            skew = weight * (6.0 * shear)
            wyz, wxz, wxy = skew * syz, skew * sxz, skew * sxy
            shares.append(x_scatter(t, [
                {"DSS": wxx, "SDS": wxy, "SSD": wxz},
                {"DSS": wxy, "SDS": wyy, "SSD": wyz},
                {"DSS": wxz, "SDS": wyz, "SSD": wzz},
            ], stores))
        leave(shares, stores)
        flush(stores)
        return 0

    def sweep_one(low, high):
        lax.fori_loop(low, high, stage_one, 0)
        stores = []
        nodes_one(high - 1, stores)
        flush(stores)

    start_one(W)
    sweep_one(W, W + BX - 1)
    for copy in first + later_own + later:
        copy.wait_send()
    unpack_parts(later, 0, 2)
    sweep_one(W + BX - 1, NP - 1)
    for copy in sums1:
        copy.wait_recv()
    total = src1[...]
    for n in range(len(plane)):
        total = total + land1[n]
    src2[...] = total
    learn(2)
    for n, d in enumerate(ring):
        send(src2, land2.at[n], d, (s2, r2), n, sums2)

    start_one(0)
    sweep_one(0, W + 1)

    def apply_sweep(ref, first_plane, last_plane, node):
        clear_carry()
        for t in range(UNITS):
            for c in range(3):
                for i, value in enumerate(full_transform(ref, c, first_plane, t)):
                    carry_t[t, 4 * c + i] = value

        def nodes(e, stores):
            for t, applied in enumerate(take_up()):
                free = raw[e, 0, unit_rows(t), :]
                for c in range(3):
                    node(c, e, t, free, applied[c], stores)

        def body(e, _):
            stores, shares = [], []
            nodes(e - 1, stores)
            for t in range(UNITS):
                modes = []
                for c in range(3):
                    new = full_transform(ref, c, e + 1, t)
                    old = [carry_t[t, 4 * c + i] for i in range(4)]
                    stores += [(carry_t, (t, 4 * c + i), value) for i, value in enumerate(new)]
                    modes.append(element_modes(old, new))
                forces = element_forces(modes, mod_e[e, unit_rows(t), :])
                shares.append(x_scatter(t, forces, stores))
            leave(shares, stores)
            flush(stores)
            return 0

        lax.fori_loop(first_plane, last_plane, body, 0)
        stores = []
        nodes(last_plane - 1, stores)
        flush(stores)

    def node_two(c, e, t, free, applied, stores):
        cells = unit_rows(t)
        d = v0[e, c, cells, :]
        r = rhs[e, c, cells, :] - (free * applied + (1.0 - free) * d)
        new = (rho_one * rho_zero) * d + (2.0 * rho_one / delta) * r
        stores += [(rhs, (e, c, cells), r), (v1, (e, c, cells), new)]
        put_node(stores, fv1, c, e, t, free * new)

    apply_sweep(fv0, 1, NP - 2, node_two)

    def node_three(c, e, t, free, applied, stores):
        cells = unit_rows(t)
        d = v1[e, c, cells, :]
        r = rhs[e, c, cells, :] - (free * applied + (1.0 - free) * d)
        new = (rho_two * rho_one) * d + (2.0 * rho_two / delta) * r
        value = v0[e, c, cells, :] + d + new
        stores.append((adj, (e, c, cells), value))
        put_node(stores, fadj, c, e, t, value)

    apply_sweep(fv1, 2, NP - 3, node_three)

    for t in range(UNITS):
        carry_p[t, 0] = zero
        for c in range(3):
            for i, value in enumerate(full_transform(fadj, c, W - 1, t)):
                carry_t[t, 4 * c + i] = value
            for i, value in enumerate(full_transform(fld, c, W - 1, t)):
                carry_t[t, 12 + 4 * c + i] = value

    def stage_four(e, _):
        stores, shares = [], []
        for t in range(UNITS):
            modes = []
            for ref, base in ((fld, 12), (fadj, 0)):
                group = []
                for c in range(3):
                    new = full_transform(ref, c, e + 1, t)
                    old = [carry_t[t, base + 4 * c + i] for i in range(4)]
                    stores += [(carry_t, (t, base + 4 * c + i), value) for i, value in enumerate(new)]
                    group.append(element_modes(old, new))
                modes.append(group if base == 0 else element_forces(group, 1.0))
            work = None
            for f, a in zip(*modes):
                for k, value in f.items():
                    work = a[k] * value if work is None else work + a[k] * value
            g = lead[e, unit_rows(t), :] - grow[e, unit_rows(t), :] * work
            share = g + carry_p[t, 0]
            stores.append((carry_p, (t, 0), g))
            put_shifted(shifted, 0, t, share)
            shares.append(share)
        for t, share in enumerate(shares):
            share = share + get_shifted(shifted, 0, t)
            stores.append((sens, (e, unit_rows(t)), share + z_prev(share)))
        flush(stores)
        return 0

    lax.fori_loop(W - 1, W + BX, stage_four, 0)

    for c in range(4):
        for p in range(BX):
            main, ends = ((sens.at[W + p], sens[W + p, 24:32, :]) if c == 3 else (adj.at[W + p, c], adj[W + p, c, 24:32, :]))
            for t in range(3):
                base = GROUP * t
                value = jnp.where(lane8 < 4, pltpu.roll(ends, (128 - 16 - base) % 128, 1), main[8 * t : 8 * t + 8, :])
                merged[c, p, 8 * t : 8 * t + 8, :] = jnp.where(
                    lane8 >= 124, pltpu.roll(ends, (120 - base) % 128, 1), value
                )

    for copy in sums1:
        copy.wait_send()
    for copy in sums2:
        copy.wait_recv()
    total = src2[...]
    for n in range(len(ring)):
        total = total + land2[n]
    total = jnp.sum(jnp.sum(total, axis=0, keepdims=True), axis=1, keepdims=True)
    mean = total * (1.0 / float(BX * BY * BZ * sizes[0] * sizes[1] * sizes[2]))
    aggregate = jnp.sqrt(jnp.sqrt(jnp.sqrt(mean)))
    scale = jnp.broadcast_to(aggregate / (8.0 * mean), (8, 128))
    share = scale * 0.125
    for p in range(BX):
        for h in (0, 8):
            sens_out[p, h : h + 8, :] = share * merged[3, p, h + 4 : h + 12, :]
            for c in range(3):
                adj_out[c, p, h : h + 8, :] = scale * merged[c, p, h + 4 : h + 12, :]

    for copy in sums2:
        copy.wait_send()


def hand_over(adj_in, sens_in, adj_out, sens_out, sems):
    copies = [pltpu.make_async_copy(adj_in, adj_out, sems.at[0]), pltpu.make_async_copy(sens_in, sens_out, sems.at[1])]
    for copy in copies:
        copy.start()
    for copy in copies:
        copy.wait()


def local(sizes, displacement, density, solid, material, fixed):
    plane, ring = partners(sizes)
    f32, i32 = jnp.float32, jnp.int32
    vm = pltpu.VMEM
    dma = pltpu.SemaphoreType.DMA
    node, paired = (NP, 3, 40, 128), (NP, 2, 3, ROWS, 128)
    element = (NP, 32, 128)
    tile = (8, 128)
    messages = len(HALO) + 3
    scratch = [
        vm((3, BX, BY, BZ), f32), vm((BX, BY, BZ), f32), vm((BX, BY, BZ), i32), vm((BX, BY, BZ), i32), vm((BX, BY, BZ), i32),
        vm((6, BX, BY, BZ), f32), vm((6, 2, 8, 128), f32), vm((6, 2, 8, 128), f32),
        vm((16, 128), f32), vm((16, 128), f32), vm(tile, f32), vm(tile, f32), vm((16, 128), f32),
        vm((2, 6, BX, BY, BZ), f32), vm((3, 2, 6, 2, 8, 128), f32), vm((3, 2, 16, 128), f32), vm((3, 2, 2, 8, 128), f32),
        vm((4, 16, 128), f32), vm((2, 16, 128), f32),
        vm((3, 2, 24, 128), f32), vm((4, BX + 1, 24, 128), f32), vm((4, BX + 1, 24, 128), f32),
        vm((NP, 24, 128), f32), vm((NP, 2, 4, ROWS, 128), f32), vm((NP, 2, 40, 128), f32),
        vm(element, f32), vm(element, f32), vm(element, f32),
        vm(node, f32), vm(node, f32), vm(paired, f32), vm(node, f32), vm(paired, f32), vm(node, f32), vm(paired, f32),
        vm(element, f32), vm((4, BX, 24, 128), f32), vm((6, ROWS, 128), f32), vm((24, 8, 128), f32),
        vm((UNITS, 24, 8, 128), f32), vm((UNITS, 12, 8, 128), f32),
        vm(tile, f32), vm((len(plane), 8, 128), f32), vm(tile, f32), vm((len(ring), 8, 128), f32),
        dma((5,)), dma((messages,)), dma((messages,)),
        dma((len(plane),)), dma((len(plane),)), dma((len(ring),)), dma((len(ring),)),
        pltpu.SemaphoreType.REGULAR((len(ROUNDS),)),
    ]
    outs = (jax.ShapeDtypeStruct((3, BX, BY, BZ), f32), jax.ShapeDtypeStruct((BX, BY, BZ), f32))
    results = pl.pallas_call(
        functools.partial(kernel, sizes),
        out_shape=outs,
        in_specs=[pl.BlockSpec(memory_space=pltpu.HBM)] * 5,
        out_specs=(pl.BlockSpec(memory_space=pltpu.VMEM), pl.BlockSpec(memory_space=pltpu.VMEM)),
        scratch_shapes=scratch,
        compiler_params=pltpu.CompilerParams(
            collective_id=0, has_side_effects=True, vmem_limit_bytes=40 * 1024 * 1024
        ),
    )(*[pltpu.with_memory_space_constraint(x, pltpu.HBM) for x in (displacement, density, solid, material, fixed)])
    return pl.pallas_call(
        hand_over,
        out_shape=outs,
        in_specs=[pl.BlockSpec(memory_space=pl.ANY)] * 2,
        out_specs=(pl.BlockSpec(memory_space=pltpu.HBM), pl.BlockSpec(memory_space=pltpu.HBM)),
        scratch_shapes=[dma((2,))],
    )(*[pltpu.with_memory_space_constraint(x, pltpu.VMEM) for x in results])


def solution(mesh):
    sizes = tuple(mesh.shape[a] for a in AXES)
    field = P(*AXES)
    vector = P(None, *AXES)
    return jax.shard_map(
        functools.partial(local, sizes),
        mesh=mesh,
        in_specs=(vector, field, field, field, field),
        out_specs=(vector, field),
        check_vma=False,
    )
```

```python
import functools
import itertools

import jax
import jax.numpy as jnp
import numpy as np
from jax import lax
from jax.experimental import pallas as pl
from jax.experimental.pallas import tpu as pltpu
from jax.sharding import PartitionSpec as P

POISSON = 0.3
VOID_FLOOR = 0.001
MODULI = (1.0, 0.7, 0.45, 0.25)
MESH = pl.DeviceIdType.MESH
AXES = ("gx", "gy", "gz")

BX, BY, BZ = 4, 16, 128
W = 4
NP = BX + 2 * W
ROWS = 56
UNITS = 4
GROUP = 24


def lame_pair():
    first = POISSON / ((1.0 + POISSON) * (1.0 - 2.0 * POISSON))
    shear = 1.0 / (2.0 * (1.0 + POISSON))
    return (first, shear)


def corner_signs():
    return [(2 * a - 1, 2 * b - 1, 2 * c - 1) for a in (0, 1) for b in (0, 1) for c in (0, 1)]


def element_table():
    first, shear = lame_pair()
    elastic = np.zeros((6, 6))
    elastic[:3, :3] = first
    for index in range(3):
        elastic[index, index] += 2.0 * shear
        elastic[index + 3, index + 3] = shear
    point = 1.0 / np.sqrt(3.0)
    matrix = np.zeros((24, 24))
    for xi in (-point, point):
        for eta in (-point, point):
            for zeta in (-point, point):
                strain = np.zeros((6, 24))
                for index, signs in enumerate(corner_signs()):
                    sa, sb, sc = signs
                    gradx = 2.0 * sa * (1 + sb * eta) * (1 + sc * zeta) / 8.0
                    grady = 2.0 * sb * (1 + sa * xi) * (1 + sc * zeta) / 8.0
                    gradz = 2.0 * sc * (1 + sa * xi) * (1 + sb * eta) / 8.0
                    strain[0, index] = gradx
                    strain[1, 8 + index] = grady
                    strain[2, 16 + index] = gradz
                    strain[3, 8 + index] = gradz
                    strain[3, 16 + index] = grady
                    strain[4, index] = gradz
                    strain[4, 16 + index] = gradx
                    strain[5, index] = grady
                    strain[5, 8 + index] = gradx
                matrix += strain.T @ elastic @ strain / 8.0
    return matrix


def chebyshev_constants():
    rowsum = float(np.max(np.sum(np.abs(element_table()), axis=1)))
    upper = max(2.0, 8.0 * max(MODULI) * rowsum)
    lower = upper / 20.0
    theta = (upper + lower) / 2.0
    delta = (upper - lower) / 2.0
    sigma = theta / delta
    rho_zero = 1.0 / sigma
    rho_one = 1.0 / (2.0 * sigma - rho_zero)
    rho_two = 1.0 / (2.0 * sigma - rho_one)
    return (theta, delta, rho_zero, rho_one, rho_two)


HALO = [d for d in itertools.product((-1, 0, 1), repeat=3) if d != (0, 0, 0)]
FIRST = [(-1, -1, -1), (0, -1, -1), (-1, 0, -1), (-1, -1, 0), (-1, 0, 0), (0, 0, -1), (0, -1, 0)]
REST = [d for d in HALO if d not in FIRST or d[2] == 0]
REST.sort(key=lambda d: (d[1] != 0 or d[2] != 0, d[0] != 0, d[2] != 0))
LATER = [d for d in HALO if d not in FIRST]


def partners(sizes):
    nx, ny, nz = sizes

    def far(d):
        return sum(min(o % n, -o % n) for o, n in zip(d, sizes))

    plane = [(a, 0, c) for a in range(nx) for c in range(nz) if (a, c) != (0, 0)]
    ring = [(0, b, 0) for b in range(1, ny)]
    return sorted(plane, key=far, reverse=True), sorted(ring, key=far, reverse=True)


ROUNDS = [
    [d for d in HALO if d[1] == 0] + [(0, 1, 0), (0, -1, 0)],
    [(2, 0, 0), (-2, 0, 0), (0, 2, 0), (0, -2, 0)],
    [(0, 4, 0), (0, -4, 0)],
]


def z_next(x):
    return pltpu.roll(x, 127, 1)


def z_prev(x):
    return pltpu.roll(x, 1, 1)


def unit_rows(t):
    return slice(8 * t, 8 * t + 8)


def put_node(stores, ref, comp, plane, t, value):
    follow = z_next(value)
    first = 32 if t == 3 else 8 * t
    for kind, x in enumerate((value + follow, follow - value)):
        stores.append((ref, (plane, kind, comp, slice(first, first + 8)), x))
        if t == 3:
            stores.append((ref, (plane, kind, comp, slice(40, 48)), pltpu.roll(x, 128 - GROUP, 1)))


def node_rows(ref, kind, comp, plane, t):
    first = 32 if t == 3 else 8 * t
    return ref[plane, kind, comp, first : first + 8, :], ref[plane, kind, comp, first + 1 : first + 9, :]


def full_transform(ref, comp, plane, t):
    s, sn = node_rows(ref, 0, comp, plane, t)
    d, dn = node_rows(ref, 1, comp, plane, t)
    return [s + sn, d + dn, sn - s, dn - d]


def central_transform(ref, comp, plane, t):
    return full_transform(ref, comp, plane, t)[:3]


def central_gradients(old, new):
    return [new[0] - old[0], old[2] + new[2], old[1] + new[1]]


def stress_of(grads):
    first, shear = lame_pair()
    exx, eyy, ezz = grads[0][0], grads[1][1], grads[2][2]
    base = first * (exx + eyy + ezz)
    sxx, syy, szz = base + 2.0 * shear * exx, base + 2.0 * shear * eyy, base + 2.0 * shear * ezz
    syz = shear * (grads[1][2] + grads[2][1])
    sxz = shear * (grads[0][2] + grads[2][0])
    sxy = shear * (grads[0][1] + grads[1][0])
    return sxx, syy, szz, syz, sxz, sxy


def unit_of(s):
    sxx, syy, szz, syz, sxz, sxy = s
    return (
        sxx * sxx + syy * syy + szz * szz - sxx * syy - syy * szz - szz * sxx
        + 3.0 * (syz * syz + sxz * sxz + sxy * sxy)
    )


def element_modes(old, new):
    ss, sd, ds, dd = zip(old, new)
    return {
        "DSS": ss[1] - ss[0], "SSD": sd[0] + sd[1], "DSD": sd[1] - sd[0], "SDS": ds[0] + ds[1],
        "DDS": ds[1] - ds[0], "SDD": dd[0] + dd[1], "DDD": dd[1] - dd[0],
    }


def element_forces(modes, modulus):
    first, shear = lame_pair()
    u, v, w = modes
    exx, eyy, ezz = u["DSS"], v["SDS"], w["SSD"]
    normal, direct, slide = modulus * (first / 16.0), modulus * (shear / 8.0), modulus * (shear / 16.0)
    base = normal * (exx + eyy + ezz)
    sxx, syy, szz = base + direct * exx, base + direct * eyy, base + direct * ezz
    syz = slide * (v["SSD"] + w["SDS"])
    sxz = slide * (u["SSD"] + w["DSS"])
    sxy = slide * (u["SDS"] + v["DSS"])
    own, cross = modulus * ((first + 3.0 * shear) / 48.0), modulus * (first / 48.0)
    twist, cube = modulus * (shear / 48.0), modulus * ((first + 4.0 * shear) / 144.0)

    def pair(a, b):
        return own * a + cross * b, cross * a + own * b

    u_xy, w_yz = pair(u["DDS"], w["SDD"])
    u_xz, v_yz = pair(u["DSD"], v["SDD"])
    v_xy, w_xz = pair(v["DDS"], w["DSD"])
    every = u["SDD"] + v["DSD"] + w["DDS"]
    return [
        {"DSS": sxx, "SDS": sxy, "SSD": sxz, "DDS": u_xy, "DSD": u_xz,
         "SDD": twist * (every + u["SDD"]), "DDD": cube * u["DDD"]},
        {"DSS": sxy, "SDS": syy, "SSD": syz, "DDS": v_xy, "SDD": v_yz,
         "DSD": twist * (every + v["DSD"]), "DDD": cube * v["DDD"]},
        {"DSS": sxz, "SDS": syz, "SSD": szz, "SDD": w_yz, "DSD": w_xz,
         "DDS": twist * (every + w["DDS"]), "DDD": cube * w["DDD"]},
    ]


def put_shifted(ref, index, t, value):
    if t < 3:
        ref[index, 8 * t + 1 : 8 * t + 9, :] = value
    else:
        ref[index, 33:41, :] = value
        ref[index, 25:33, :] = pltpu.roll(value, GROUP, 1)


def get_shifted(ref, index, t):
    first = 32 if t == 3 else 8 * t
    return ref[index, first : first + 8, :]


def kernel(sizes, disp_in, dens_in, solid_in, mat_in, fixed_in, adj_out, sens_out,
           disp_v, dens_v, solid_v, mat_v, fixed_v, own, ylow, yhigh, zlow, zhigh, zlow_y, zhigh_y, yfirst,
           rx, ry, rz, ryz, rxf, ryf, strip, tm, tn, rows, fld, raw, mod_e, grow, lead, rhs, v0, fv0, v1, fv1, adj, fadj, sens,
           merged, shifted, lowers,
           carry_t, carry_p, src1, land1, src2, land2, in_sem, send_sem, recv_sem, s1, r1, s2, r2, known):
    position = [lax.axis_index(a) for a in AXES]

    def at(d):
        return tuple(lax.rem(p + (o % n), n) if o % n else p for p, o, n in zip(position, d, sizes))

    plane, ring = partners(sizes)
    theta, delta, rho_zero, rho_one, rho_two = chebyshev_constants()

    loads = [
        pltpu.make_async_copy(src, dst, in_sem.at[n])
        for n, (src, dst) in enumerate(
            ((disp_in, disp_v), (fixed_in, fixed_v), (dens_in, dens_v), (mat_in, mat_v), (solid_in, solid_v))
        )
    ]
    for copy in loads:
        copy.start()
    barrier = pltpu.get_barrier_semaphore()
    greeted = LATER + FIRST
    for d in greeted:
        pl.semaphore_signal(barrier, inc=1, device_id=at(d), device_id_type=MESH)
    for copy in loads:
        copy.wait()

    free = 1.0 - fixed_v[...].astype(jnp.float32)
    own[4] = free
    own[3] = dens_v[...]
    for c in range(3):
        own[c] = disp_v[c] * free
    material = mat_v[...]
    scale_class = jnp.zeros(material.shape, jnp.float32)
    for index in range(4):
        scale_class = scale_class + jnp.where(material == index, MODULI[index], 0.0).astype(jnp.float32)
    own[5] = scale_class * (VOID_FLOOR + (1.0 - VOID_FLOOR) * solid_v[...].astype(jnp.float32))

    lane16 = lax.broadcasted_iota(jnp.int32, (16, 128), 1)
    lane8 = lax.broadcasted_iota(jnp.int32, (8, 128), 1)

    def pack_lanes(first_lane, offset, ref, ref_y):
        packed = jnp.zeros((16, 128), jnp.float32)
        for f in range(6):
            for p in range(BX):
                place = 4 * (BX * f + p) + offset
                shift = (place - first_lane) % 128
                block = own[f, p]
                packed = jnp.where(lane16 < place, packed, pltpu.roll(block, shift, 1) if shift else block)
        ref[...] = packed
        ref_y[0:4, :] = packed[0:4]
        ref_y[4:8, :] = packed[12:16]

    pack_lanes(0, 0, zlow, zlow_y)
    for f in range(4):
        for p in range(BX):
            yfirst[BX * f + p : BX * f + p + 1, :] = own[f, p, 0:1, :]

    pack_lanes(124, 4, zhigh, zhigh_y)
    for f in range(6):
        for p in range(BX):
            half = 4 * (p % 2)
            ylow[f, p // 2, half : half + 4, :] = own[f, p, 0:4, :]
            yhigh[f, p // 2, half : half + 4, :] = own[f, p, 12:16, :]
    pl.semaphore_wait(barrier, len(greeted))

    def send(src, dst, d, sems, n, group):
        copy = pltpu.make_async_remote_copy(
            src_ref=src, dst_ref=dst, send_sem=sems[0].at[n], recv_sem=sems[1].at[n],
            device_id=at(d), device_id_type=MESH,
        )
        copy.start()
        group.append(copy)

    halo_sems = (send_sem, recv_sem)
    first, later = [], []
    for n, (dx, dy, dz) in enumerate(FIRST):
        sx = 1 - dx
        if dz:
            src, dst = (zlow_y, ryz.at[sx, 1, 1]) if dy else (zlow, rz.at[sx, 1])
        else:
            src, dst = (yfirst, ryf.at[sx - 1]) if dy else (own.at[pl.ds(0, 4), 0], rxf)
        send(src, dst, (dx, dy, dz), halo_sems, n, first)

    def tell(n):
        for d in ROUNDS[n]:
            pl.semaphore_signal(known.at[n], inc=1, device_id=at(d), device_id_type=MESH)

    def learn(n):
        pl.semaphore_wait(known.at[n], len(ROUNDS[n]))

    later_own = []
    for n, (dx, dy, dz) in enumerate(REST):
        sx, sy, sz = 1 - dx, (1 - dy) // 2, (1 - dz) // 2
        if dz == 0 and dy == 0:
            src, dst = own, rx.at[sx // 2]
        elif dz == 0:
            src, dst = (yhigh if dy > 0 else ylow), ry.at[sx, sy]
        elif dy == 0:
            src, dst = (zhigh if dz > 0 else zlow), rz.at[sx, sz]
        else:
            src, dst = (zhigh_y if dz > 0 else zlow_y), ryz.at[sx, sy, sz]
        send(src, dst, (dx, dy, dz), halo_sems, len(FIRST) + n, later if dx else later_own)
        if n == 7:
            tell(0)
    learn(0)
    tell(1)

    zero = jnp.zeros((8, 128), jnp.float32)

    def clear(p, _):
        for kind in range(2):
            for c in range(4):
                fld[p, kind, c, 24:32, :] = zero
            for c in range(3):
                fv0[p, kind, c, 24:32, :] = zero
                fv1[p, kind, c, 24:32, :] = zero
                fadj[p, kind, c, 24:32, :] = zero
        return 0

    for i in range(6):
        shifted[i, 0:8, :] = zero
    for i in range(24):
        lowers[i] = zero
        shifted[i % 6, 8 + 8 * (i // 6) : 16 + 8 * (i // 6), :] = zero
    lax.fori_loop(0, NP, clear, 0)

    def inside(axis, o):
        if o == 0:
            return 1.0
        edge = 0 if o < 0 else sizes[axis] - 1
        return jnp.where(position[axis] == edge, 0.0, 1.0).astype(jnp.float32)

    for copy in first:
        copy.wait_recv()
    in_x, in_y, in_z = inside(0, 1), inside(1, 1), inside(2, 1)
    strips = [(rz[1, 1] * in_z, ryz[1, 1, 1] * (in_y * in_z)),
              (rz[2, 1] * (in_x * in_z), ryz[2, 1, 1] * (in_x * in_y * in_z))]
    for f in range(4):
        for p in range(BX + 1):
            far = p // BX
            group = 4 * (BX * f + p % BX)
            block = rxf[f] * in_x if far else own[f, p]
            line = ryf[far, BX * f + p % BX : BX * f + p % BX + 1, :] * (in_y * in_x if far else in_y)
            line = jnp.broadcast_to(line, (8, 128))
            tm[f, p, 0:16, :] = block
            tm[f, p, 16:24, :] = line
            z16, z8 = strips[far]
            tn[f, p, 0:16, :] = jnp.where(lane16 == 127, pltpu.roll(z16, 127 - group, 1), z_next(block))
            tn[f, p, 16:24, :] = jnp.where(lane8 == 127, pltpu.roll(z8, 127 - group, 1), z_next(line))

    partial = zero
    for start in (0, 8):
        old = None
        for p in range(BX + 1):
            new = []
            for f in range(4):
                a, an = tm[f, p, start : start + 8, :], tn[f, p, start : start + 8, :]
                b, bn = tm[f, p, start + 1 : start + 9, :], tn[f, p, start + 1 : start + 9, :]
                s, sn = a + b, an + bn
                new.append([s + sn, sn - s, (b - a) + (bn - an)])
            if old is not None:
                grads = [[0.25 * g for g in central_gradients(old[c], new[c])] for c in range(3)]
                rho = (old[3][0] + new[3][0]) * 0.125
                modulus = rho * rho * rho * own[5, p - 1, start : start + 8, :]
                q = modulus * modulus * unit_of(stress_of(grads))
                q = q * q
                partial = partial + q * q
            old = new
    src1[...] = partial
    sums1, sums2 = [], []
    learn(1)
    tell(2)
    for n, d in enumerate(plane):
        send(src1, land1.at[n], d, (s1, r1), n, sums1)

    lane24 = lax.broadcasted_iota(jnp.int32, (24, 128), 1)
    even_half = lane24 % 8 < 4
    def merge_strips(sx):
        sides = []
        for sz in range(2):
            f_xz = inside(0, sx - 1) * inside(2, 2 * sz - 1)
            strip[sx, sz, 0:4, :] = ryz[sx, 0, sz, 4:8, :] * (f_xz * inside(1, -1))
            strip[sx, sz, 4:20, :] = rz[sx, sz] * f_xz
            strip[sx, sz, 20:24, :] = ryz[sx, 1, sz, 0:4, :] * (f_xz * inside(1, 1))
            sides.append(strip[sx, sz])
        below, above = sides
        strip[sx, 0] = jnp.where(even_half, above, below)
        strip[sx, 1] = jnp.where(even_half, below, above)

    def flush(stores):
        for ref, index, value in stores:
            ref[index] = value

    def unpack(f, is_raw, parts):
        for sx in parts:
            fx = inside(0, sx - 1)
            for p in range(BX):
                q = BX * sx + p
                half = 4 * (p % 2)
                rows[q, 4:20, :] = own[f, p] if sx == 1 else rx[sx // 2, f, p] * fx
                rows[q, 0:4, :] = ry[sx, 0, f, p // 2, half : half + 4, :] * (fx * inside(1, -1))
                rows[q, 20:24, :] = ry[sx, 1, f, p // 2, half : half + 4, :] * (fx * inside(1, 1))
        for sx in parts:
            stores = []
            for p in range(BX):
                q = BX * sx + p
                group = 4 * (BX * f + p)
                units, ends = [], None
                for t in range(3):
                    base = GROUP * t
                    chunk = rows[q, 8 * t : 8 * t + 8, :]
                    outer = strip[sx, p % 2, 8 * t : 8 * t + 8, :]
                    value = jnp.where(lane8 < base + 16, pltpu.roll(outer, lax.rem(base + 8 + 128 - group, 128), 1),
                                      pltpu.roll(chunk, base + 16, 1))
                    value = jnp.where(lane8 < base + 8, pltpu.roll(chunk, base + 8, 1), value)
                    ends = value if ends is None else jnp.where(lane8 < base, ends, value)
                    units.append(chunk)
                units.append(ends)
                for t, value in enumerate(units):
                    if is_raw:
                        stores.append((raw, (q, f - 4, unit_rows(t)), value))
                    else:
                        put_node(stores, fld, f, q, t, value)
            flush(stores)

    def unpack_parts(copies, *parts):
        for copy in copies:
            copy.wait_recv()
        for sx in parts:
            merge_strips(sx)

        def nodes(f, _):
            unpack(f, False, parts)
            return 0

        def elements(f, _):
            unpack(f, True, parts)
            return 0

        lax.fori_loop(0, 4, nodes, 0)
        lax.fori_loop(4, 6, elements, 0)

    unpack_parts(later_own, 1)

    kinds = ("SS", "SD", "DS", "DD")

    def x_scatter(t, forces, stores):
        result = []
        for c in range(3):
            by = {}
            for i, k in enumerate(kinds):
                s, d = forces[c].get("S" + k), forces[c].get("D" + k)
                if s is None and d is None:
                    continue
                if s is None:
                    by[k] = carry_p[t, 4 * c + i] - d
                    upper = d
                elif d is None:
                    by[k] = carry_p[t, 4 * c + i] + s
                    upper = s
                else:
                    by[k] = carry_p[t, 4 * c + i] + (s - d)
                    upper = s + d
                stores.append((carry_p, (t, 4 * c + i), upper))
            result.append(by)
        return result

    def leave(shares, stores):
        for t, group in enumerate(shares):
            for c, by in enumerate(group):
                for i, k in enumerate("SD"):
                    s, d = by["S" + k], by.get("D" + k)
                    lower, upper = (s, s) if d is None else (s - d, s + d)
                    stores.append((lowers, 6 * t + 2 * c + i, lower))
                    index = 2 * c + i
                    if t < 3:
                        stores.append((shifted, (index, slice(8 * t + 1, 8 * t + 9)), upper))
                    else:
                        stores.append((shifted, (index, slice(33, 41)), upper))
                        stores.append((shifted, (index, slice(25, 33)), pltpu.roll(upper, GROUP, 1)))

    def take_up():
        result = []
        for t in range(UNITS):
            values = []
            for c in range(3):
                s, d = [lowers[6 * t + 2 * c + i] + get_shifted(shifted, 2 * c + i, t) for i in range(2)]
                values.append((s - d) + z_prev(s + d))
            result.append(values)
        return result

    def clear_carry():
        for i in range(12):
            for t in range(UNITS):
                carry_p[t, i] = zero

    def start_one(p):
        clear_carry()
        for t in range(UNITS):
            for c in range(3):
                for i, value in enumerate(central_transform(fld, c, p, t)):
                    carry_t[t, 4 * c + i] = value
            s, sn = node_rows(fld, 0, 3, p, t)
            carry_t[t, 12] = s + sn

    def nodes_one(e, stores):
        for t, load in enumerate(take_up()):
            cells = unit_rows(t)
            free = raw[e, 0, cells, :]
            for c in range(3):
                r = free * load[c]
                d = r * (1.0 / theta)
                stores += [(rhs, (e, c, cells), r), (v0, (e, c, cells), d)]

    def pair_up(source, made, e, stores, masked=True):
        for t in range(UNITS):
            free = raw[e, 0, unit_rows(t), :]
            for c in range(3):
                value = source[e, c, unit_rows(t), :]
                put_node(stores, made, c, e, t, free * value if masked else value)

    def stage_one(e, _):
        stores, shares = [], []
        pair_up(v0, fv0, jnp.maximum(e - 2, 0), stores)
        nodes_one(jnp.maximum(e - 1, 0), stores)
        first, shear = lame_pair()
        for t in range(UNITS):
            cells = unit_rows(t)
            grads = []
            for c in range(3):
                new = central_transform(fld, c, e + 1, t)
                old = [carry_t[t, 4 * c + i] for i in range(3)]
                stores += [(carry_t, (t, 4 * c + i), value) for i, value in enumerate(new)]
                grads.append([0.25 * g for g in central_gradients(old, new)])
            s, sn = node_rows(fld, 0, 3, e + 1, t)
            mass = s + sn
            rho = (carry_t[t, 12] + mass) * 0.125
            rho_stiff = rho * rho * raw[e, 1, cells, :]
            modulus = rho_stiff * rho
            growth = 3.0 * rho_stiff
            stress = stress_of(grads)
            unit = unit_of(stress)
            square = modulus * modulus
            q = square * unit
            q3 = q * q * q
            stores += [
                (carry_t, (t, 12), mass), (mod_e, (e, cells), modulus), (grow, (e, cells), growth),
                (lead, (e, cells), growth * (8.0 * q3 * modulus * unit)),
            ]
            sxx, syy, szz, syz, sxz, sxy = stress
            weight = q3 * square
            trace = sxx + syy + szz
            hxx, hyy, hzz = 3.0 * sxx - trace, 3.0 * syy - trace, 3.0 * szz - trace
            base = first * (hxx + hyy + hzz)
            wxx = weight * (base + 2.0 * shear * hxx)
            wyy = weight * (base + 2.0 * shear * hyy)
            wzz = weight * (base + 2.0 * shear * hzz)
            skew = weight * (6.0 * shear)
            wyz, wxz, wxy = skew * syz, skew * sxz, skew * sxy
            shares.append(x_scatter(t, [
                {"DSS": wxx, "SDS": wxy, "SSD": wxz},
                {"DSS": wxy, "SDS": wyy, "SSD": wyz},
                {"DSS": wxz, "SDS": wyz, "SSD": wzz},
            ], stores))
        leave(shares, stores)
        flush(stores)
        return 0

    def sweep_one(low, high):
        lax.fori_loop(low, high, stage_one, 0)
        stores = []
        pair_up(v0, fv0, high - 2, stores)
        nodes_one(high - 1, stores)
        flush(stores)
        stores = []
        pair_up(v0, fv0, high - 1, stores)
        flush(stores)

    start_one(W)
    sweep_one(W, W + BX - 1)
    for copy in first + later_own + later:
        copy.wait_send()
    unpack_parts(later, 0, 2)
    sweep_one(W + BX - 1, NP - 1)
    for copy in sums1:
        copy.wait_recv()
    total = src1[...]
    for n in range(len(plane)):
        total = total + land1[n]
    src2[...] = total
    learn(2)
    for n, d in enumerate(ring):
        send(src2, land2.at[n], d, (s2, r2), n, sums2)

    start_one(0)
    sweep_one(0, W + 1)

    def apply_sweep(ref, first_plane, last_plane, node, source, made, masked):
        clear_carry()
        for t in range(UNITS):
            for c in range(3):
                for i, value in enumerate(full_transform(ref, c, first_plane, t)):
                    carry_t[t, 4 * c + i] = value

        def nodes(e, stores):
            for t, applied in enumerate(take_up()):
                free = raw[e, 0, unit_rows(t), :]
                for c in range(3):
                    node(c, e, t, free, applied[c], stores)

        def body(e, _):
            stores, shares = [], []
            pair_up(source, made, jnp.maximum(e - 2, 0), stores, masked)
            nodes(e - 1, stores)
            for t in range(UNITS):
                modes = []
                for c in range(3):
                    new = full_transform(ref, c, e + 1, t)
                    old = [carry_t[t, 4 * c + i] for i in range(4)]
                    stores += [(carry_t, (t, 4 * c + i), value) for i, value in enumerate(new)]
                    modes.append(element_modes(old, new))
                forces = element_forces(modes, mod_e[e, unit_rows(t), :])
                shares.append(x_scatter(t, forces, stores))
            leave(shares, stores)
            flush(stores)
            return 0

        lax.fori_loop(first_plane, last_plane, body, 0)
        stores = []
        pair_up(source, made, last_plane - 2, stores, masked)
        nodes(last_plane - 1, stores)
        flush(stores)
        stores = []
        pair_up(source, made, last_plane - 1, stores, masked)
        flush(stores)

    def node_two(c, e, t, free, applied, stores):
        cells = unit_rows(t)
        d = v0[e, c, cells, :]
        r = rhs[e, c, cells, :] - (free * applied + (1.0 - free) * d)
        new = (rho_one * rho_zero) * d + (2.0 * rho_one / delta) * r
        stores += [(rhs, (e, c, cells), r), (v1, (e, c, cells), new)]

    apply_sweep(fv0, 1, NP - 2, node_two, v1, fv1, True)

    def node_three(c, e, t, free, applied, stores):
        cells = unit_rows(t)
        d = v1[e, c, cells, :]
        r = rhs[e, c, cells, :] - (free * applied + (1.0 - free) * d)
        new = (rho_two * rho_one) * d + (2.0 * rho_two / delta) * r
        value = v0[e, c, cells, :] + d + new
        stores.append((adj, (e, c, cells), value))

    apply_sweep(fv1, 2, NP - 3, node_three, adj, fadj, False)

    for t in range(UNITS):
        carry_p[t, 0] = zero
        for c in range(3):
            for i, value in enumerate(full_transform(fadj, c, W - 1, t)):
                carry_t[t, 4 * c + i] = value
            for i, value in enumerate(full_transform(fld, c, W - 1, t)):
                carry_t[t, 12 + 4 * c + i] = value

    def stage_four(e, _):
        stores, shares = [], []
        for t in range(UNITS):
            modes = []
            for ref, base in ((fld, 12), (fadj, 0)):
                group = []
                for c in range(3):
                    new = full_transform(ref, c, e + 1, t)
                    old = [carry_t[t, base + 4 * c + i] for i in range(4)]
                    stores += [(carry_t, (t, base + 4 * c + i), value) for i, value in enumerate(new)]
                    group.append(element_modes(old, new))
                modes.append(group if base == 0 else element_forces(group, 1.0))
            work = None
            for f, a in zip(*modes):
                for k, value in f.items():
                    work = a[k] * value if work is None else work + a[k] * value
            g = lead[e, unit_rows(t), :] - grow[e, unit_rows(t), :] * work
            share = g + carry_p[t, 0]
            stores.append((carry_p, (t, 0), g))
            put_shifted(shifted, 0, t, share)
            shares.append(share)
        for t, share in enumerate(shares):
            share = share + get_shifted(shifted, 0, t)
            stores.append((sens, (e, unit_rows(t)), share + z_prev(share)))
        flush(stores)
        return 0

    lax.fori_loop(W - 1, W + BX, stage_four, 0)

    for c in range(4):
        for p in range(BX):
            main, ends = ((sens.at[W + p], sens[W + p, 24:32, :]) if c == 3 else (adj.at[W + p, c], adj[W + p, c, 24:32, :]))
            for t in range(3):
                base = GROUP * t
                value = jnp.where(lane8 < 4, pltpu.roll(ends, (128 - 16 - base) % 128, 1), main[8 * t : 8 * t + 8, :])
                merged[c, p, 8 * t : 8 * t + 8, :] = jnp.where(
                    lane8 >= 124, pltpu.roll(ends, (120 - base) % 128, 1), value
                )

    for copy in sums1:
        copy.wait_send()
    for copy in sums2:
        copy.wait_recv()
    total = src2[...]
    for n in range(len(ring)):
        total = total + land2[n]
    total = jnp.sum(jnp.sum(total, axis=0, keepdims=True), axis=1, keepdims=True)
    mean = total * (1.0 / float(BX * BY * BZ * sizes[0] * sizes[1] * sizes[2]))
    aggregate = jnp.sqrt(jnp.sqrt(jnp.sqrt(mean)))
    scale = jnp.broadcast_to(aggregate / (8.0 * mean), (8, 128))
    share = scale * 0.125
    for p in range(BX):
        for h in (0, 8):
            sens_out[p, h : h + 8, :] = share * merged[3, p, h + 4 : h + 12, :]
            for c in range(3):
                adj_out[c, p, h : h + 8, :] = scale * merged[c, p, h + 4 : h + 12, :]

    for copy in sums2:
        copy.wait_send()


def hand_over(adj_in, sens_in, adj_out, sens_out, sems):
    copies = [pltpu.make_async_copy(adj_in, adj_out, sems.at[0]), pltpu.make_async_copy(sens_in, sens_out, sems.at[1])]
    for copy in copies:
        copy.start()
    for copy in copies:
        copy.wait()


def local(sizes, displacement, density, solid, material, fixed):
    plane, ring = partners(sizes)
    f32, i32 = jnp.float32, jnp.int32
    vm = pltpu.VMEM
    dma = pltpu.SemaphoreType.DMA
    node, paired = (NP, 3, 40, 128), (NP, 2, 3, ROWS, 128)
    element = (NP, 32, 128)
    tile = (8, 128)
    messages = len(HALO) + 3
    scratch = [
        vm((3, BX, BY, BZ), f32), vm((BX, BY, BZ), f32), vm((BX, BY, BZ), i32), vm((BX, BY, BZ), i32), vm((BX, BY, BZ), i32),
        vm((6, BX, BY, BZ), f32), vm((6, 2, 8, 128), f32), vm((6, 2, 8, 128), f32),
        vm((16, 128), f32), vm((16, 128), f32), vm(tile, f32), vm(tile, f32), vm((16, 128), f32),
        vm((2, 6, BX, BY, BZ), f32), vm((3, 2, 6, 2, 8, 128), f32), vm((3, 2, 16, 128), f32), vm((3, 2, 2, 8, 128), f32),
        vm((4, 16, 128), f32), vm((2, 16, 128), f32),
        vm((3, 2, 24, 128), f32), vm((4, BX + 1, 24, 128), f32), vm((4, BX + 1, 24, 128), f32),
        vm((NP, 24, 128), f32), vm((NP, 2, 4, ROWS, 128), f32), vm((NP, 2, 40, 128), f32),
        vm(element, f32), vm(element, f32), vm(element, f32),
        vm(node, f32), vm(node, f32), vm(paired, f32), vm(node, f32), vm(paired, f32), vm(node, f32), vm(paired, f32),
        vm(element, f32), vm((4, BX, 24, 128), f32), vm((6, ROWS, 128), f32), vm((24, 8, 128), f32),
        vm((UNITS, 24, 8, 128), f32), vm((UNITS, 12, 8, 128), f32),
        vm(tile, f32), vm((len(plane), 8, 128), f32), vm(tile, f32), vm((len(ring), 8, 128), f32),
        dma((5,)), dma((messages,)), dma((messages,)),
        dma((len(plane),)), dma((len(plane),)), dma((len(ring),)), dma((len(ring),)),
        pltpu.SemaphoreType.REGULAR((len(ROUNDS),)),
    ]
    outs = (jax.ShapeDtypeStruct((3, BX, BY, BZ), f32), jax.ShapeDtypeStruct((BX, BY, BZ), f32))
    results = pl.pallas_call(
        functools.partial(kernel, sizes),
        out_shape=outs,
        in_specs=[pl.BlockSpec(memory_space=pltpu.HBM)] * 5,
        out_specs=(pl.BlockSpec(memory_space=pltpu.VMEM), pl.BlockSpec(memory_space=pltpu.VMEM)),
        scratch_shapes=scratch,
        compiler_params=pltpu.CompilerParams(
            collective_id=0, has_side_effects=True, vmem_limit_bytes=40 * 1024 * 1024
        ),
    )(*[pltpu.with_memory_space_constraint(x, pltpu.HBM) for x in (displacement, density, solid, material, fixed)])
    return pl.pallas_call(
        hand_over,
        out_shape=outs,
        in_specs=[pl.BlockSpec(memory_space=pl.ANY)] * 2,
        out_specs=(pl.BlockSpec(memory_space=pltpu.HBM), pl.BlockSpec(memory_space=pltpu.HBM)),
        scratch_shapes=[dma((2,))],
    )(*[pltpu.with_memory_space_constraint(x, pltpu.VMEM) for x in results])


def solution(mesh):
    sizes = tuple(mesh.shape[a] for a in AXES)
    field = P(*AXES)
    vector = P(None, *AXES)
    return jax.shard_map(
        functools.partial(local, sizes),
        mesh=mesh,
        in_specs=(vector, field, field, field, field),
        out_specs=(vector, field),
        check_vma=False,
    )
```
